512 devices in a mesh: dp: 32 (over x, z), resp: 16 (over y, core).
Axes of the slice: x: 4, y: 8, z: 8, core: 2. Of those that a mesh axis runs over, the one named last changes fastest.
Arguments:
- queries: bfloat16 [65536, 2560], P(('dp', 'resp')), parts along dimension 0, may hold values from -5 to 5
- keys: bfloat16 [65536, 2560], P(('dp', 'resp')), parts along dimension 0, may hold values from -5 to 5
- values: bfloat16 [65536, 2560], P(('dp', 'resp')), parts along dimension 0, may hold values from -6 to 6
- cotangent: bfloat16 [65536, 2560], P(('dp', 'resp')), parts along dimension 0, may hold values from -6 to 6
- lengths: int32 [512, 4], P(('dp', 'resp')), parts along dimension 0, may hold values from 0 to 32, as said below
- prompt_keys: bfloat16 [4096, 2560], P(('dp', 'resp')), parts along dimension 0, may hold values from -5 to 5
- prompt_values: bfloat16 [4096, 2560], P(('dp', 'resp')), parts along dimension 0, may hold values from -6 to 6
Outputs:
- query_grad: bfloat16 [65536, 2560], P(('dp', 'resp')), parts along dimension 0
- key_grad: bfloat16 [65536, 2560], P(('dp', 'resp')), parts along dimension 0
- value_grad: bfloat16 [65536, 2560], P(('dp', 'resp')), parts along dimension 0
- prompt_key_grad: bfloat16 [4096, 2560], P(('dp', 'resp')), parts along dimension 0
- prompt_value_grad: bfloat16 [4096, 2560], P(('dp', 'resp')), parts along dimension 0
The draws below stay inside these ranges and needn't reach their ends.
There are 32 independent parts, one for each index of `dp`. The reference program is written for one: setup_inputs(seed, part) draws one part's arguments, and reference() takes and returns one part's arrays. A program takes and returns all parts, laid end to end along the dimension named above; each array names one. Nothing has to cross between parts.
Inputs may be any that keep to these rules, and one draw needn't show every extreme that they name: `lengths`: each row sums to at most 128; in every draw some row sums to exactly 128; a 0 means no response.
All inputs are finite; a program needn't handle non-finite values.
Results may differ from the reference program's by a relative error of at most 0.035.
Values may be sent and summed in bfloat16 or wider, within the bound.
A program may use at most 64 MiB of HBM per device.

```python
import jax
import jax.numpy as jnp
from jax import lax

H = 20
HD = 128
RT = 128
PROMPT_DEV = 8
RPD = 4
PROMPT = 128
RESP_TOK = 2048
N_RESP = 16


def draw_queries(key, part):
    width = H * HD
    rows = RT * N_RESP
    key = jax.random.fold_in(key, 3)
    first = jax.random.fold_in(key, 0)
    result = jnp.clip(jax.random.normal(first, (rows, width), jnp.float32), -5.0, 5.0)
    return result.astype(jnp.bfloat16)


def draw_keys(key, part):
    width = H * HD
    rows = RT * N_RESP
    key = jax.random.fold_in(key, 7)
    result = jnp.clip(jax.random.normal(key, (rows, width), jnp.float32), -5.0, 5.0)
    return result.astype(jnp.bfloat16)


def draw_prompt_keys(key, part):
    width = H * HD
    rows = PROMPT_DEV * N_RESP
    key = jax.random.fold_in(key, 5)
    result = jnp.clip(jax.random.normal(key, (rows, width), jnp.float32), -5.0, 5.0)
    return result.astype(jnp.bfloat16)


def draw_lengths(key, part):
    key = jax.random.fold_in(key, 11)
    first, second, third = jax.random.split(key, 3)
    most = RT // RPD
    base = jax.random.randint(first, (N_RESP, RPD), max(1, RT // (4 * RPD)), most + 1)
    count = jax.random.randint(second, (N_RESP, 1), 1, RPD + 1)
    slot = jnp.arange(RPD)[None, :]
    result = jnp.where(slot < count, base, 0)
    full = jax.random.randint(third, (), 0, N_RESP)
    result = jnp.where((jnp.arange(N_RESP) == full)[:, None], most, result)
    return result.astype(jnp.int32)


def shard_levels(key, dims, pieces, least, top_value):
    def one(position, parts):
        heights = jax.random.uniform(jax.random.fold_in(jax.random.fold_in(key, 6), position), (parts,), jnp.float32, least / len(pieces), top_value / len(pieces))
        return jnp.repeat(jnp.exp(heights), dims[position] // parts).reshape((-1,) + (1,) * (len(dims) - position - 1))

    gain = one(*pieces[0])
    for cut in pieces[1:]:
        gain = gain * one(*cut)
    return gain


def gaussian(own_key, dims, deviation, limit, cuts=(), kind=jnp.bfloat16):
    values = deviation * jax.random.normal(own_key, dims, jnp.float32)
    if cuts:
        values = values * shard_levels(own_key, dims, cuts, -0.22, 0.18)
    return jnp.clip(values, -limit, limit).astype(kind)


def setup_inputs(seed: int = 0, part: int = 0) -> dict:
    splits = jax.random.split(jax.random.key(seed), 8)
    part_keys = jax.random.split(jax.random.fold_in(splits[7], part), 8)
    return {
        "queries": draw_queries(jax.random.fold_in(jax.random.fold_in(splits[7], part), 71), part),
        "keys": draw_keys(jax.random.fold_in(jax.random.fold_in(splits[7], part), 71), part),
        "values": gaussian(part_keys[2], (RESP_TOK, H * HD), 1.0, 6.0, ((0, 16),)),
        "cotangent": gaussian(part_keys[3], (RESP_TOK, H * HD), 1.0, 6.0, ((0, 16),)),
        "lengths": draw_lengths(jax.random.fold_in(jax.random.fold_in(splits[7], part), 71), part),
        "prompt_keys": draw_prompt_keys(jax.random.fold_in(jax.random.fold_in(splits[7], part), 71), part),
        "prompt_values": gaussian(part_keys[6], (PROMPT, H * HD), 1.0, 6.0, ((0, 16),)),
    }


def slot_layout(length_row, slots):
    ends = jnp.cumsum(length_row).astype(jnp.int32)
    place = jnp.arange(slots, dtype=jnp.int32)
    segment = jnp.sum((place[:, None] >= ends[None, :]).astype(jnp.int32), axis=1).astype(jnp.int32)
    live = place < ends[-1]
    return place, segment, live


def one_block(items, prompt_keys, prompt_values):
    query, key_self, value_self, cotan, length_row = items
    slots, width = query.shape
    heads = width // HD
    scale = HD ** -0.5
    prompt_rows = prompt_keys.shape[0]
    place, segment, live = slot_layout(length_row, slots)
    allowed_self = (segment[:, None] == segment[None, :]) & (place[None, :] <= place[:, None]) & live[:, None] & live[None, :]
    allowed = jnp.concatenate([jnp.ones((slots, prompt_rows), dtype=bool), allowed_self], axis=1)
    all_keys = jnp.concatenate([prompt_keys, key_self], axis=0).reshape(-1, heads, HD).astype(jnp.float32)
    all_values = jnp.concatenate([prompt_values, value_self], axis=0).reshape(-1, heads, HD).astype(jnp.float32)
    query3 = query.reshape(slots, heads, HD).astype(jnp.float32)
    cot3 = cotan.reshape(slots, heads, HD).astype(jnp.float32)
    scores = jnp.einsum('qhd,khd->hqk', query3, all_keys) * scale
    scores = jnp.where(allowed[None], scores, -jnp.inf)
    top = jnp.max(scores, axis=2, keepdims=True)
    lse = top + jnp.log(jnp.sum(jnp.exp(scores - top), axis=2, keepdims=True))
    prob = jnp.where(live[None, :, None], jnp.exp(scores - lse), 0.0)
    prob_b = prob.astype(jnp.bfloat16).astype(jnp.float32)
    attn_out = jnp.einsum('hqk,khd->qhd', prob_b, all_values).astype(jnp.bfloat16).astype(jnp.float32)
    delta = jnp.transpose(jnp.sum(cot3 * attn_out, axis=2))[:, :, None]
    dprob = jnp.einsum('qhd,khd->hqk', cot3, all_values)
    dscore = (prob * (dprob - delta)).astype(jnp.bfloat16).astype(jnp.float32)
    query_grad = (jnp.einsum('hqk,khd->qhd', dscore, all_keys) * scale).reshape(slots, width)
    key_all = (jnp.einsum('hqk,qhd->khd', dscore, query3) * scale).reshape(-1, width)
    value_all = jnp.einsum('hqk,qhd->khd', prob_b, cot3).reshape(-1, width)
    return (query_grad.astype(jnp.bfloat16), key_all[prompt_rows:].astype(jnp.bfloat16),
            value_all[prompt_rows:].astype(jnp.bfloat16), key_all[:prompt_rows].astype(jnp.bfloat16),
            value_all[:prompt_rows].astype(jnp.bfloat16))


def reference(queries, keys, values, cotangent, lengths, prompt_keys, prompt_values):
    width = queries.shape[1]
    blocks = (queries.reshape(N_RESP, RT, width), keys.reshape(N_RESP, RT, width),
              values.reshape(N_RESP, RT, width), cotangent.reshape(N_RESP, RT, width), lengths)
    query_grad, key_grad, value_grad, prompt_parts_k, prompt_parts_v = lax.map(
        lambda items: one_block(items, prompt_keys, prompt_values), blocks)
    prompt_key_grad = jnp.sum(prompt_parts_k.astype(jnp.float32), axis=0).astype(jnp.bfloat16)
    prompt_value_grad = jnp.sum(prompt_parts_v.astype(jnp.float32), axis=0).astype(jnp.bfloat16)
    return (query_grad.reshape(-1, width), key_grad.reshape(-1, width), value_grad.reshape(-1, width),
            prompt_key_grad, prompt_value_grad)
```

```python
import functools

import jax
import jax.numpy as jnp
from jax import lax
from jax.experimental import pallas as pl
from jax.experimental.pallas import tpu as pltpu
from jax.sharding import PartitionSpec as P

HD = 128
CHIPS = 8
HPC = 5
SCALE = HD ** (-0.5)
LOG2E = 1.4426950408889634
MASKED = -1e30
MESH = pl.DeviceIdType.MESH
NT = (((1,), (1,)), ((), ()))
NN = (((1,), (0,)), ((), ()))
TN = (((0,), (0,)), ((), ()))
F32 = jnp.float32
BF16 = jnp.bfloat16


def mm(a, b, dims):
    return lax.dot_general(a, b, dims, preferred_element_type=F32)


SLOT = {0: 0, 2: 1, -2: 2, 1: 3, -1: 4, 3: 5, -3: 6, 4: 7, -4: 7}


def half(ch, way):
    cut = HPC // 2 + (HPC % 2) * (ch % 2)
    return pl.ds(0, cut * HD) if way == 1 else pl.ds(cut * HD, (HPC - cut) * HD)


def kernel(
    nc,
    len_hbm, q_hbm, k_hbm, v_hbm, co_hbm, pk_hbm, pv_hbm,
    dq_ref, dk_ref, dv_ref, pg_ref,
    len_ref, pk_ref, pv_ref, q_ref, co_ref, ka_ref, va_ref,
    gat_ref, part_ref, sib_ref, tx_ref, mid_ref, end_ref,
    bias_ref, e_ref, dp_ref, ds_ref, stat_ref,
    in_sem,
    ag_send, ag_recv, ag2_send, ag2_recv,
    rs_send, rs_recv, rs2_send, rs2_recv,
):
    width = HPC * HD
    me = lax.axis_index("resp")
    y = me // 2
    core = lax.rem(me, 2)
    sibling = 2 * y + (1 - core)

    def away(offset):
        return 2 * lax.rem(y + CHIPS + offset, CHIPS) + core

    def remote(src, dst, send, recv, to):
        return pltpu.make_async_remote_copy(
            src_ref=src, dst_ref=dst, send_sem=send, recv_sem=recv,
            device_id={"resp": to}, device_id_type=MESH,
        )

    lower = pl.ds(128, 128)
    loads = [
        pltpu.make_async_copy(pk_hbm, pk_ref, in_sem.at[0]),
        pltpu.make_async_copy(pv_hbm, pv_ref, in_sem.at[1]),
        pltpu.make_async_copy(q_hbm, q_ref, in_sem.at[2]),
        pltpu.make_async_copy(k_hbm, ka_ref.at[lower], in_sem.at[3]),
        pltpu.make_async_copy(co_hbm, co_ref, in_sem.at[4]),
        pltpu.make_async_copy(v_hbm, va_ref.at[lower], in_sem.at[5]),
        pltpu.make_async_copy(len_hbm, len_ref, in_sem.at[6]),
    ]
    for load in loads:
        load.start()

    barrier = pltpu.get_barrier_semaphore()
    for other in (sibling, away(1), away(-1), away(2), away(-2)):
        pl.semaphore_signal(barrier, inc=1, device_id={"resp": other}, device_id_type=MESH)

    loads[0].wait()
    loads[1].wait()
    own = jnp.concatenate([pk_ref[...].astype(F32), pv_ref[...].astype(F32)], axis=0).astype(BF16)
    for ch in range(nc):
        gat_ref[ch, 0, 0] = own[:, ch * width:(ch + 1) * width]

    pl.semaphore_wait(barrier, 5)

    def ag_copy(ch, way, kind):
        n = 2 if kind != 2 else 0 if way == 1 else 1
        if kind <= 2:
            src, dst = gat_ref.at[ch, 0, 0], gat_ref.at[ch, 0, SLOT[-way * kind]]
        else:
            src, dst = gat_ref.at[ch, 0, SLOT[-way * 2]], gat_ref.at[ch, 0, SLOT[-way * kind]]
            if kind == 4:
                src, dst = src.at[:, half(ch, way)], dst.at[:, half(ch, way)]
        return remote(src, dst, ag_send.at[ch], ag_recv.at[ch, n],
                      away(way * (2 if kind in (2, 4) else 1)))

    def ag_far(ch):
        for way in (1, -1):
            ag_copy(ch, way, 2).start()

    def ag_near(ch):
        for way in (1, -1):
            ag_copy(ch, way, 1).start()

    def ag_second(ch):
        for way in (1, -1):
            ag_copy(ch, way, 2).wait_recv()
            ag_copy(ch, way, 4).start()
            ag_copy(ch, way, 3).start()

    def ag_pair(ch):
        return remote(gat_ref.at[ch, 0], gat_ref.at[ch, 1], ag2_send.at[ch], ag2_recv.at[ch], sibling)

    def ag_third(ch):
        rest = gat_ref.at[ch, 0, pl.ds(3, 5)]
        remote(rest, rest, ag_send.at[ch], ag_recv.at[ch, 2], sibling).wait_recv()
        ag_pair(ch).start()

    def ag_sent(ch):
        every = gat_ref.at[ch, 0, pl.ds(1, 7)]
        remote(every, every, ag_send.at[ch], ag_recv.at[ch, 2], sibling).wait_send()
        ag_pair(ch).wait_send()

    ag_far(0)
    ag_near(0)
    for ch in range(1, min(nc, 3)):
        ag_far(ch)

    loads[6].wait()
    ends = [len_ref[0, 0]]
    for r in range(1, 4):
        ends.append(ends[-1] + len_ref[0, r])
    key_at = lax.broadcasted_iota(jnp.int32, (128, 128), 0)
    query_at = lax.broadcasted_iota(jnp.int32, (128, 128), 1)

    def segment_of(place):
        return sum((place >= end).astype(jnp.int32) for end in ends)

    allowed = (segment_of(key_at) == segment_of(query_at)) & (key_at <= query_at)
    allowed = allowed & (query_at < ends[3])
    bias_ref[...] = jnp.where(allowed, 0.0, MASKED).astype(F32)
    live = lax.broadcasted_iota(jnp.int32, (1, 128), 1) < ends[3]

    def in_turn(ch, first, rest):
        ahead = first(ch * HPC)
        for h in range(ch * HPC, (ch + 1) * HPC):
            now = ahead
            if h + 1 < (ch + 1) * HPC:
                ahead = first(h + 1)
            rest(h, *now)

    def columns(h):
        return pl.ds(h * HD, HD)

    def own_keys(ch):
        def first(h):
            cols = columns(h)
            return mm(ka_ref[lower, cols], q_ref[:, cols], NT), mm(va_ref[lower, cols], co_ref[:, cols], NT)

        def rest(h, s, dp):
            s = s * (SCALE * LOG2E) + bias_ref[...]
            m = jnp.max(s, axis=0, keepdims=True)
            e = jnp.exp2(s - m)
            e_ref[h] = e
            dp_ref[h] = dp
            stat_ref[h, 0:1] = m
            stat_ref[h, 1:2] = jnp.sum(e, axis=0, keepdims=True)
            stat_ref[h, 2:3] = jnp.sum(e * dp, axis=0, keepdims=True)

        in_turn(ch, first, rest)

    def prompt_keys(ch):
        def inner(h):
            return pl.ds((h - ch * HPC) * HD, HD)

        def first(h):
            cols = columns(h)
            both = gat_ref[ch, :, :, :, inner(h)].reshape(16, 16, HD).astype(F32)
            kp = both[:, :8].reshape(128, HD).astype(BF16)
            vp = both[:, 8:].reshape(128, HD).astype(BF16)
            ka_ref[0:128, cols] = kp
            return mm(kp, q_ref[:, cols], NT), mm(vp, co_ref[:, cols], NT)

        def rest(h, s, dp):
            cols = columns(h)
            s = s * (SCALE * LOG2E)
            m_own = stat_ref[h, 0:1]
            m = jnp.maximum(jnp.max(s, axis=0, keepdims=True), m_own)
            e = jnp.exp2(s - m)
            a = jnp.exp2(m_own - m)
            total = jnp.sum(e, axis=0, keepdims=True) + a * stat_ref[h, 1:2]
            inv = jnp.where(live, 1.0 / total, 0.0)
            delta = (jnp.sum(e * dp, axis=0, keepdims=True) + a * stat_ref[h, 2:3]) * inv
            p = e * inv
            ds = (p * (dp - delta)).astype(BF16)
            ds_ref[h] = ds
            stat_ref[h, 3:4] = a * inv
            stat_ref[h, 4:5] = delta
            gk = (mm(ds, q_ref[:, cols], NN) * SCALE).reshape(16, 8, HD)
            gv = mm(p.astype(BF16), co_ref[:, cols], NN).reshape(16, 8, HD)
            part_ref[ch, :, :, :, inner(h)] = (
                jnp.concatenate([gk, gv], axis=1).astype(BF16).reshape(2, CHIPS, 16, HD))

        in_turn(ch, first, rest)

    def gradients(ch):
        def first(h):
            p = e_ref[h] * stat_ref[h, 3:4]
            ds = (p * (dp_ref[h] - stat_ref[h, 4:5])).astype(BF16)
            return p.astype(BF16), ds

        def rest(h, p, ds):
            cols = columns(h)
            dv_ref[:, cols] = mm(p, co_ref[:, cols], NN).astype(BF16)
            dk_ref[:, cols] = (mm(ds, q_ref[:, cols], NN) * SCALE).astype(BF16)
            both = jnp.concatenate([ds_ref[h], ds], axis=0)
            dq_ref[:, cols] = (mm(both, ka_ref[:, cols], TN) * SCALE).astype(BF16)

        in_turn(ch, first, rest)

    def rs_pair(ch):
        return remote(part_ref.at[ch, 1], sib_ref.at[ch], rs2_send.at[ch], rs2_recv.at[ch], sibling)

    def rs_copy(ch, way, kind):
        w = 0 if way == 1 else 1
        src = tx_ref.at[ch, 4 * w + kind - 1]
        if kind <= 2:
            dst, sem = end_ref.at[ch, 2 * w + kind - 1], rs_recv.at[ch, 0]
        else:
            dst, sem = mid_ref.at[ch, w, kind - 3], rs_recv.at[ch, 2 * w + kind - 2]
        if kind == 4:
            src, dst = src.at[:, half(ch, way)], dst.at[:, half(ch, way)]
        return remote(src, dst, rs_send.at[ch], sem, away(way * (2 if kind in (2, 4) else 1)))

    def rs_sent(ch):
        every = tx_ref.at[ch, pl.ds(0, 7)]
        remote(every, every, rs_send.at[ch], rs_recv.at[ch, 0], sibling).wait_send()
        rs_pair(ch).wait_send()

    def chip_sum(ch, offset):
        slot = SLOT[offset]
        return part_ref[ch, 0, slot].astype(F32) + sib_ref[ch, slot].astype(F32)

    def rs_first(ch):
        rs_pair(ch).wait_recv()
        far = chip_sum(ch, 4)
        for w, way in enumerate((1, -1)):
            cols = half(ch, way)
            tx_ref[ch, 4 * w + 3, :, cols] = far[:, cols.start:cols.start + cols.size].astype(BF16)
            rs_copy(ch, way, 4).start()
            for kind in (3, 1):
                tx_ref[ch, 4 * w + kind - 1] = chip_sum(ch, way * kind).astype(BF16)
                rs_copy(ch, way, kind).start()

    def rs_second(ch):
        for w, way in enumerate((1, -1)):
            cols = half(ch, way)
            rs_copy(ch, way, 3).wait_recv()
            rs_copy(ch, way, 4).wait_recv()
            total = chip_sum(ch, way * 2) + mid_ref[ch, w, 0].astype(F32)
            tx_ref[ch, 4 * w + 1] = total.astype(BF16)
            part = total[:, cols.start:cols.start + cols.size]
            tx_ref[ch, 4 * w + 1, :, cols] = (
                part + mid_ref[ch, w, 1, :, cols].astype(F32)).astype(BF16)
            rs_copy(ch, way, 2).start()

    def rs_third(ch):
        last = end_ref.at[ch]
        remote(last, last, rs_send.at[ch], rs_recv.at[ch, 0], sibling).wait_recv()
        total = chip_sum(ch, 0)
        for n in range(4):
            total = total + end_ref[ch, n].astype(F32)
        pg_ref[:, ch * width:(ch + 1) * width] = total.astype(BF16)

    for n in (2, 3, 4, 5):
        loads[n].wait()
    def prompt_step(ch):
        ag_pair(ch).wait_recv()
        prompt_keys(ch)
        rs_pair(ch).start()

    for step, ch in (
        (own_keys, 0), (ag_second, 0), (ag_near, 1), (ag_far, 3),
        (own_keys, 1), (ag_second, 1), (ag_near, 2),
        (own_keys, 2), (ag_second, 2), (ag_near, 3), (ag_third, 0),
        (own_keys, 3), (ag_second, 3), (ag_third, 1), (prompt_step, 0),
        (ag_third, 2), (prompt_step, 1),
        (rs_first, 0), (ag_third, 3), (prompt_step, 2),
        (rs_first, 1), (prompt_step, 3),
        (rs_first, 2), (rs_second, 0), (gradients, 0),
        (rs_first, 3), (rs_second, 1), (gradients, 1),
        (rs_second, 2), (gradients, 2),
        (rs_second, 3), (gradients, 3),
        (ag_sent, 0), (ag_sent, 1), (ag_sent, 2), (ag_sent, 3),
        (rs_third, 0), (rs_third, 1), (rs_third, 2),
        (rs_sent, 0), (rs_sent, 1), (rs_sent, 2), (rs_third, 3), (rs_sent, 3),
    ):
        if ch < nc:
            step(ch)


def finish(dq_in, dk_in, dv_in, pg_in, dq, dk, dv, gk, gv, gk_ref, gv_ref, sem):
    copies = []
    for n, (src, dst) in enumerate(((dq_in, dq), (dk_in, dk), (dv_in, dv))):
        for part in range(4):
            rows = pl.ds(part * 32, 32)
            copies.append(pltpu.make_async_copy(src.at[rows], dst.at[rows], sem.at[n, part]))
    for copy in copies:
        copy.start()
    both = pg_in[...].astype(F32)
    gk_ref[...] = both[:8].astype(BF16)
    gv_ref[...] = both[8:].astype(BF16)
    for n, (src, dst) in enumerate(((gk_ref, gk), (gv_ref, gv))):
        copies.append(pltpu.make_async_copy(src, dst, sem.at[3, n]))
        copies[-1].start()
    for copy in copies:
        copy.wait()


def per_device(queries, keys, values, cotangent, lengths, prompt_keys, prompt_values):
    slots, width = queries.shape
    n_heads = width // HD
    nc = n_heads // HPC
    cw = HPC * HD
    anywhere = pl.BlockSpec(memory_space=pl.ANY)
    vmem = pl.BlockSpec(memory_space=pltpu.VMEM)
    dma = pltpu.SemaphoreType.DMA
    big = jax.ShapeDtypeStruct((slots, width), BF16)
    small = jax.ShapeDtypeStruct((8, width), BF16)
    dq, dk, dv, pg = pl.pallas_call(
        functools.partial(kernel, nc),
        out_shape=(pltpu.VMEM((slots, width), BF16),) * 3 + (pltpu.VMEM((16, width), BF16),),
        in_specs=[pl.BlockSpec(memory_space=pltpu.HBM)] * 7,
        out_specs=(vmem,) * 4,
        scratch_shapes=[
            pltpu.SMEM((1, 4), jnp.int32),
            pltpu.VMEM((8, width), BF16),
            pltpu.VMEM((8, width), BF16),
            pltpu.VMEM((slots, width), BF16),
            pltpu.VMEM((slots, width), BF16),
            pltpu.VMEM((256, width), BF16),
            pltpu.VMEM((256, width), BF16),
            pltpu.VMEM((nc, 2, CHIPS, 16, cw), BF16),
            pltpu.VMEM((nc, 2, CHIPS, 16, cw), BF16),
            pltpu.VMEM((nc, CHIPS, 16, cw), BF16),
            pltpu.VMEM((nc, 8, 16, cw), BF16),
            pltpu.VMEM((nc, 2, 2, 16, cw), BF16),
            pltpu.VMEM((nc, 4, 16, cw), BF16),
            pltpu.VMEM((128, 128), F32),
            pltpu.VMEM((n_heads, 128, 128), F32),
            pltpu.VMEM((n_heads, 128, 128), F32),
            pltpu.VMEM((n_heads, 128, 128), BF16),
            pltpu.VMEM((n_heads, 8, 128), F32),
            dma((7,)),
            dma((nc,)), dma((nc, 3)), dma((nc,)), dma((nc,)),
            dma((nc,)), dma((nc, 5)), dma((nc,)), dma((nc,)),
        ],
        compiler_params=pltpu.CompilerParams(
            collective_id=0, has_side_effects=True, vmem_limit_bytes=40 * 1024 * 1024
        ),
    )(*(
        pltpu.with_memory_space_constraint(x, pltpu.HBM)
        for x in (lengths, queries, keys, values, cotangent, prompt_keys, prompt_values)
    ))
    return pl.pallas_call(
        finish,
        out_shape=(big, big, big, small, small),
        in_specs=[anywhere, anywhere, anywhere, vmem],
        out_specs=(anywhere,) * 5,
        scratch_shapes=[pltpu.VMEM((8, width), BF16), pltpu.VMEM((8, width), BF16), dma((4, 4))],
        compiler_params=pltpu.CompilerParams(vmem_limit_bytes=8 * 1024 * 1024),
    )(*(pltpu.with_memory_space_constraint(x, pltpu.VMEM) for x in (dq, dk, dv, pg)))


def solution(mesh):
    spec = P(("dp", "resp"), None)
    return jax.shard_map(
        per_device, mesh=mesh, in_specs=(spec,) * 7, out_specs=(spec,) * 5, check_vma=False
    )
```

```python
import functools

import jax
import jax.numpy as jnp
from jax import lax
from jax.experimental import pallas as pl
from jax.experimental.pallas import tpu as pltpu
from jax.sharding import PartitionSpec as P

HD = 128
CHIPS = 8
SCALE = HD ** (-0.5)
LOG2E = 1.4426950408889634
MASKED = -1e30
MESH = pl.DeviceIdType.MESH
NT = (((1,), (1,)), ((), ()))
NN = (((1,), (0,)), ((), ()))
TN = (((0,), (0,)), ((), ()))
F32 = jnp.float32
BF16 = jnp.bfloat16


def mm(a, b, dims):
    return lax.dot_general(a, b, dims, preferred_element_type=F32)


SLOT = {0: 0, 2: 1, -2: 2, 1: 3, -1: 4, 3: 5, -3: 6, 4: 7, -4: 7}


def chunks_of(heads):
    if heads == 10:
        return (0, 2, 5, 8, 10)
    return tuple(range(0, heads, 2)) + (heads,)


def kernel(
    cuts,
    len_hbm, q_hbm, k_hbm, v_hbm, co_hbm, pk_hbm, pv_hbm,
    out_ref, pg_ref,
    len_ref, pk_ref, pv_ref, q_ref, co_ref, ka_ref, va_ref,
    gat_ref, other_ref, part_ref, mid_ref, tx_ref, end_ref,
    bias_ref, e_ref, dp_ref, ds_ref, stat_ref, grad_ref,
    in_sem, swap_send, swap_recv, own_sem, grad_sem,
    ag_send, ag_recv, rs_send, rs_recv, rs_own,
):
    nc = len(cuts) - 1
    wide = cuts[-1] * HD
    me = lax.axis_index("resp")
    y = me // 2
    core = lax.rem(me, 2)
    sibling = 2 * y + (1 - core)
    mine = pl.ds(pl.multiple_of(core * wide, wide), wide)
    theirs = pl.ds(pl.multiple_of((1 - core) * wide, wide), wide)

    def away(offset, other=0):
        return 2 * lax.rem(y + CHIPS + offset, CHIPS) + (1 - core if other else core)

    def remote(src, dst, send, recv, to):
        return pltpu.make_async_remote_copy(
            src_ref=src, dst_ref=dst, send_sem=send, recv_sem=recv,
            device_id={"resp": to}, device_id_type=MESH,
        )

    def span(ch):
        return pl.ds(cuts[ch] * HD, (cuts[ch + 1] - cuts[ch]) * HD)

    def half(ch, way):
        lo, hi = cuts[ch], cuts[ch + 1]
        cut = lo + (hi - lo + ch % 2) // 2
        return pl.ds(lo * HD, (cut - lo) * HD) if way == 1 else pl.ds(cut * HD, (hi - cut) * HD)

    key_rows = (pl.ds(0, 128), pl.ds(256, 128))
    prompt_rows = pl.ds(128, 128)

    loads = [
        pltpu.make_async_copy(pk_hbm, pk_ref, in_sem.at[0]),
        pltpu.make_async_copy(pv_hbm, pv_ref, in_sem.at[1]),
        pltpu.make_async_copy(len_hbm, len_ref, in_sem.at[2]),
        pltpu.make_async_copy(k_hbm.at[:, mine], ka_ref.at[key_rows[0]], in_sem.at[3]),
        pltpu.make_async_copy(q_hbm.at[:, mine], q_ref.at[0], in_sem.at[4]),
        pltpu.make_async_copy(v_hbm.at[:, mine], va_ref.at[0], in_sem.at[5]),
        pltpu.make_async_copy(co_hbm.at[:, mine], co_ref.at[0], in_sem.at[6]),
    ]
    for load in loads:
        load.start()

    barrier = pltpu.get_barrier_semaphore()
    partners = [sibling] + [away(o, other) for o in (1, -1, 2, -2) for other in (0, 1)]
    for partner in partners:
        pl.semaphore_signal(barrier, inc=1, device_id={"resp": partner}, device_id_type=MESH)

    loads[0].wait()
    loads[1].wait()
    own = jnp.concatenate([pk_ref[...].astype(F32), pv_ref[...].astype(F32)], axis=0)
    first_core = core == 0
    gat_ref[0, 0] = jnp.where(first_core, own[:, :wide], own[:, wide:]).astype(BF16)
    other_ref[...] = jnp.where(first_core, own[:, wide:], own[:, :wide]).astype(BF16)

    pl.semaphore_wait(barrier, len(partners))

    def ag_send_own(ch, kind):
        cols = span(ch)
        for way in (1, -1):
            sem = 2 if kind == 1 else 0 if way == 1 else 1
            for other in (0, 1):
                src = other_ref.at[:, cols] if other else gat_ref.at[0, 0, :, cols]
                dst = gat_ref.at[SLOT[-way * kind], other, :, cols]
                remote(src, dst, ag_send.at[ch], ag_recv.at[ch, sem], away(way * kind, other)).start()

    def ag_far(ch):
        ag_send_own(ch, 2)

    def ag_near(ch):
        ag_send_own(ch, 1)

    def ag_second(ch):
        for way in (1, -1):
            slot = SLOT[-way * 2]
            block = gat_ref.at[slot, :, :, span(ch)]
            remote(block, block, ag_send.at[ch], ag_recv.at[ch, 0 if way == 1 else 1],
                   sibling).wait_recv()
            cols = half(ch, way)
            remote(gat_ref.at[slot, :, :, cols], gat_ref.at[SLOT[4], :, :, cols],
                   ag_send.at[ch], ag_recv.at[ch, 2], away(way * 2)).start()
            remote(block, gat_ref.at[SLOT[-way * 3], :, :, span(ch)],
                   ag_send.at[ch], ag_recv.at[ch, 2], away(way)).start()

    def ag_third(ch):
        rest = gat_ref.at[pl.ds(3, 5), :, :, span(ch)]
        remote(rest, rest, ag_send.at[ch], ag_recv.at[ch, 2], sibling).wait_recv()

    def ag_sent(ch):
        every = gat_ref.at[pl.ds(1, 7), :, :, span(ch)]
        remote(every, every, ag_send.at[ch], ag_recv.at[ch, 2], sibling).wait_send()

    own_block = remote(other_ref, gat_ref.at[0, 1], own_sem.at[0], own_sem.at[1], sibling)
    swaps = [
        remote(src, dst, swap_send.at[n], swap_recv.at[n], sibling)
        for n, (src, dst) in enumerate((
            (k_hbm.at[:, theirs], ka_ref.at[key_rows[1]]),
            (q_hbm.at[:, theirs], q_ref.at[1]),
            (v_hbm.at[:, theirs], va_ref.at[1]),
            (co_hbm.at[:, theirs], co_ref.at[1]),
            (bias_ref.at[0], bias_ref.at[1]),
        ))
    ]
    ag_far(0)
    ag_near(0)
    for ch in range(1, nc):
        ag_far(ch)
    own_block.start()
    for swap in swaps[:4]:
        swap.start()

    loads[2].wait()
    ends = [len_ref[0, 0]]
    for r in range(1, 4):
        ends.append(ends[-1] + len_ref[0, r])
    key_at = lax.broadcasted_iota(jnp.int32, (128, 128), 0)
    query_at = lax.broadcasted_iota(jnp.int32, (128, 128), 1)

    def segment_of(place):
        return sum((place >= end).astype(jnp.int32) for end in ends)

    allowed = (segment_of(key_at) == segment_of(query_at)) & (key_at <= query_at)
    allowed = allowed & (query_at < ends[3])
    bias_ref[0, 0:128] = jnp.where(allowed, 0.0, MASKED).astype(F32)
    bias_ref[0, 128:136] = jnp.where(query_at[0:8] < ends[3], 1.0, 0.0).astype(F32)
    swaps[4].start()
    for load in loads[3:]:
        load.wait()

    def in_turn(items, first, rest):
        ahead = first(*items[0])
        for n, item in enumerate(items):
            now = ahead
            if n + 1 < len(items):
                ahead = first(*items[n + 1])
            rest(*item, *now)

    def columns(h):
        return pl.ds(h * HD, HD)

    def heads(ch):
        return range(cuts[ch], cuts[ch + 1])

    def own_keys(ch, b):
        def first(h):
            cols = columns(h)
            return (mm(ka_ref[key_rows[b], cols], q_ref[b, :, cols], NT),
                    mm(va_ref[b, :, cols], co_ref[b, :, cols], NT))

        def rest(h, s, dp):
            s = s * (SCALE * LOG2E) + bias_ref[b, 0:128]
            m = jnp.max(s, axis=0, keepdims=True)
            e = jnp.exp2(s - m)
            e_ref[h, b] = e
            dp_ref[h, b] = dp
            lanes = pl.ds(b * 128, 128)
            stat_ref[h, 0:1, lanes] = m
            stat_ref[h, 1:2, lanes] = jnp.sum(e, axis=0, keepdims=True)
            stat_ref[h, 2:3, lanes] = jnp.sum(e * dp, axis=0, keepdims=True)

        in_turn([(h,) for h in heads(ch)], first, rest)

    def own_keys_0(ch):
        own_keys(ch, 0)

    def own_keys_1(ch):
        if ch == 0:
            for swap in swaps:
                swap.wait_recv()
        own_keys(ch, 1)

    def prompt_keys(ch):
        if ch == 0:
            own_block.wait_recv()
        ag_third(ch)
        live = jnp.concatenate([bias_ref[0, 128:129], bias_ref[1, 128:129]], axis=1)

        def first(h):
            cols = columns(h)
            both = gat_ref[:, :, :, cols].reshape(16, 16, HD).astype(F32)
            kp = both[:, :8].reshape(128, HD).astype(BF16)
            vp = both[:, 8:].reshape(128, HD).astype(BF16)
            ka_ref[prompt_rows, cols] = kp
            return (mm(kp, q_ref[:, :, cols].reshape(256, HD), NT),
                    mm(vp, co_ref[:, :, cols].reshape(256, HD), NT))

        def rest(h, s, dp):
            cols = columns(h)
            s = s * (SCALE * LOG2E)
            m_own = stat_ref[h, 0:1]
            m = jnp.maximum(jnp.max(s, axis=0, keepdims=True), m_own)
            e = jnp.exp2(s - m)
            a = jnp.exp2(m_own - m)
            total = jnp.sum(e, axis=0, keepdims=True) + a * stat_ref[h, 1:2]
            inv = live / total
            delta = (jnp.sum(e * dp, axis=0, keepdims=True) + a * stat_ref[h, 2:3]) * inv
            p = e * inv
            ds = (p * (dp - delta)).astype(BF16)
            ds_ref[h] = ds
            stat_ref[h, 3:4] = a * inv
            stat_ref[h, 4:5] = delta
            gk = mm(ds, q_ref[:, :, cols].reshape(256, HD), NN).reshape(16, 8, HD)
            gv = mm(p.astype(BF16), co_ref[:, :, cols].reshape(256, HD), NN).reshape(16, 8, HD)
            part_ref[:, :, :, cols] = (
                jnp.concatenate([gk, gv], axis=1).astype(BF16).reshape(CHIPS, 2, 16, HD))

        in_turn([(h,) for h in heads(ch)], first, rest)

    def give_back(ch):
        lo, size = cuts[ch] * HD, (cuts[ch + 1] - cuts[ch]) * HD
        at = pl.ds(pl.multiple_of(core * wide + lo, HD), size)
        return remote(grad_ref.at[:, :, span(ch)], out_ref.at[:, :, at],
                      grad_sem.at[0, ch], grad_sem.at[1, ch], sibling)

    def gradients(ch):
        def first(h, b):
            lanes = pl.ds(b * 128, 128)
            p = e_ref[h, b] * stat_ref[h, 3:4, lanes]
            ds = (p * (dp_ref[h, b] - stat_ref[h, 4:5, lanes])).astype(BF16)
            return p.astype(BF16), ds

        def rest(h, b, p, ds):
            cols = columns(h)
            dv = mm(p, co_ref[b, :, cols], NN).astype(BF16)
            dk = (mm(ds, q_ref[b, :, cols], NN) * SCALE).astype(BF16)
            dsp = ds_ref[h, :, pl.ds(b * 128, 128)]
            both = jnp.concatenate([ds, dsp] if b == 0 else [dsp, ds], axis=0)
            dq = (mm(both, ka_ref[pl.ds(b * 128, 256), cols], TN) * SCALE).astype(BF16)
            for n, grad in enumerate((dq, dk, dv)):
                if b == 0:
                    at = pl.ds(pl.multiple_of(core * wide + h * HD, HD), HD)
                    out_ref[n, :, at] = grad
                else:
                    grad_ref[n, :, cols] = grad

        in_turn([(h, b) for b in (1, 0) for h in heads(ch)], first, rest)
        give_back(ch).start()

    def end_at(kind, way, other):
        return 4 * other + 2 * (kind - 1) + (0 if way == 1 else 1)

    def rs_last(ch, kind, way, src):
        cols = span(ch)
        for other in (0, 1):
            remote(src.at[other, :, cols], end_ref.at[end_at(kind, way, other), :, cols],
                   rs_send.at[ch], rs_recv.at[ch, 0], away(way * kind, other)).start()

    def rs_mid(ch, kind, way):
        w = 0 if way == 1 else 1
        cols = half(ch, way) if kind == 4 else span(ch)
        return remote(part_ref.at[SLOT[way * kind], :, :, cols], mid_ref.at[w, kind - 3, :, :, cols],
                      rs_send.at[ch], rs_recv.at[ch, 2 * w + kind - 2],
                      away(way * (2 if kind == 4 else 1)))

    def rs_near(ch):
        cols = span(ch)
        return remote(part_ref.at[0, 1, :, cols], end_ref.at[8, :, cols],
                      rs_own.at[ch], rs_recv.at[ch, 0], sibling)

    def rs_first(ch):
        for way in (1, -1):
            rs_mid(ch, 4, way).start()
            rs_mid(ch, 3, way).start()
        for way in (1, -1):
            rs_last(ch, 1, way, part_ref.at[SLOT[way]])
        rs_near(ch).start()

    def rs_second(ch):
        cols = span(ch)
        for w, way in enumerate((1, -1)):
            some = half(ch, way)
            rs_mid(ch, 3, way).wait_recv()
            rs_mid(ch, 4, way).wait_recv()
            for other in (0, 1):
                total = part_ref[SLOT[way * 2], other, :, cols].astype(F32)
                total = total + mid_ref[w, 0, other, :, cols].astype(F32)
                tx_ref[w, other, :, cols] = total.astype(BF16)
                at = some.start - cols.start
                total = total[:, at:at + some.size] + mid_ref[w, 1, other, :, some].astype(F32)
                tx_ref[w, other, :, some] = total.astype(BF16)
            rs_last(ch, 2, way, tx_ref.at[w])

    def rs_third(ch):
        cols = span(ch)
        last = end_ref.at[:, :, cols]
        remote(last, last, rs_send.at[ch], rs_recv.at[ch, 0], sibling).wait_recv()
        same = part_ref[0, 0, :, cols].astype(F32)
        for n in range(4):
            same = same + end_ref[n, :, cols].astype(F32)
        other = end_ref[4, :, cols].astype(F32)
        for n in range(5, 9):
            other = other + end_ref[n, :, cols].astype(F32)
        for at, total in ((core, same), (1 - core, other)):
            total = jnp.concatenate([total[:8] * SCALE, total[8:]], axis=0)
            pg_ref[at, :, cols] = total.astype(BF16)

    def rs_sent(ch):
        every = part_ref.at[pl.ds(0, 7), :, :, span(ch)]
        remote(every, every, rs_send.at[ch], rs_recv.at[ch, 0], sibling).wait_send()
        rs_near(ch).wait_send()

    def swapped(ch):
        if ch == 0:
            own_block.wait_send()
            for swap in swaps:
                swap.wait_send()
        ag_sent(ch)

    def given(ch):
        give_back(ch).wait()

    for step, ch in (
        (own_keys_0, 0), (ag_second, 0), (ag_near, 1),
        (own_keys_0, 1), (ag_second, 1), (ag_near, 2),
        (own_keys_0, 2), (ag_second, 2), (ag_near, 3),
        (own_keys_0, 3), (ag_second, 3),
        (own_keys_1, 0), (own_keys_1, 1), (prompt_keys, 0), (rs_first, 0),
        (own_keys_1, 2), (prompt_keys, 1), (rs_first, 1),
        (own_keys_1, 3), (prompt_keys, 2), (rs_first, 2), (rs_second, 0),
        (prompt_keys, 3), (rs_first, 3), (rs_second, 1),
        (gradients, 0), (rs_second, 2), (gradients, 1), (rs_second, 3),
        (gradients, 2), (gradients, 3),
        (swapped, 0), (swapped, 1), (swapped, 2), (swapped, 3),
        (rs_third, 0), (rs_third, 1), (rs_third, 2),
        (rs_sent, 0), (rs_sent, 1), (rs_sent, 2), (given, 0), (given, 1), (given, 2),
        (rs_third, 3), (rs_sent, 3), (given, 3),
    ):
        if ch < nc:
            step(ch)


def finish(out_in, pg_in, dq, dk, dv, gk, gv, gk_ref, gv_ref, sem):
    copies = []
    for n, dst in enumerate((dq, dk, dv)):
        for part in range(4):
            rows = pl.ds(part * 32, 32)
            copies.append(pltpu.make_async_copy(out_in.at[n, rows], dst.at[rows], sem.at[n, part]))
    for copy in copies:
        copy.start()
    both = jnp.concatenate([pg_in[0].astype(F32), pg_in[1].astype(F32)], axis=1)
    gk_ref[...] = both[:8].astype(BF16)
    gv_ref[...] = both[8:].astype(BF16)
    for n, (src, dst) in enumerate(((gk_ref, gk), (gv_ref, gv))):
        copies.append(pltpu.make_async_copy(src, dst, sem.at[3, n]))
        copies[-1].start()
    for copy in copies:
        copy.wait()


def per_device(queries, keys, values, cotangent, lengths, prompt_keys, prompt_values):
    slots, width = queries.shape
    heads = width // HD // 2
    wide = heads * HD
    cuts = chunks_of(heads)
    nc = len(cuts) - 1
    anywhere = pl.BlockSpec(memory_space=pl.ANY)
    vmem = pl.BlockSpec(memory_space=pltpu.VMEM)
    dma = pltpu.SemaphoreType.DMA
    big = jax.ShapeDtypeStruct((slots, width), BF16)
    small = jax.ShapeDtypeStruct((8, width), BF16)
    out, pg = pl.pallas_call(
        functools.partial(kernel, cuts),
        out_shape=(pltpu.VMEM((3, slots, width), BF16), pltpu.VMEM((2, 16, wide), BF16)),
        in_specs=[pl.BlockSpec(memory_space=pltpu.HBM)] * 7,
        out_specs=(vmem,) * 2,
        scratch_shapes=[
            pltpu.SMEM((1, 4), jnp.int32),
            pltpu.VMEM((8, width), BF16),
            pltpu.VMEM((8, width), BF16),
            pltpu.VMEM((2, slots, wide), BF16),
            pltpu.VMEM((2, slots, wide), BF16),
            pltpu.VMEM((384, wide), BF16),
            pltpu.VMEM((2, slots, wide), BF16),
            pltpu.VMEM((CHIPS, 2, 16, wide), BF16),
            pltpu.VMEM((16, wide), BF16),
            pltpu.VMEM((CHIPS, 2, 16, wide), BF16),
            pltpu.VMEM((2, 2, 2, 16, wide), BF16),
            pltpu.VMEM((2, 2, 16, wide), BF16),
            pltpu.VMEM((9, 16, wide), BF16),
            pltpu.VMEM((2, 136, 128), F32),
            pltpu.VMEM((heads, 2, 128, 128), F32),
            pltpu.VMEM((heads, 2, 128, 128), F32),
            pltpu.VMEM((heads, 128, 256), BF16),
            pltpu.VMEM((heads, 8, 256), F32),
            pltpu.VMEM((3, slots, wide), BF16),
            dma((7,)), dma((5,)), dma((5,)), dma((2,)), dma((2, nc)),
            dma((nc,)), dma((nc, 3)), dma((nc,)), dma((nc, 5)), dma((nc,)),
        ],
        compiler_params=pltpu.CompilerParams(
            collective_id=0, has_side_effects=True, vmem_limit_bytes=40 * 1024 * 1024
        ),
    )(*(
        pltpu.with_memory_space_constraint(x, pltpu.HBM)
        for x in (lengths, queries, keys, values, cotangent, prompt_keys, prompt_values)
    ))
    return pl.pallas_call(
        finish,
        out_shape=(big, big, big, small, small),
        in_specs=[anywhere, vmem],
        out_specs=(anywhere,) * 5,
        scratch_shapes=[pltpu.VMEM((8, width), BF16), pltpu.VMEM((8, width), BF16), dma((4, 4))],
        compiler_params=pltpu.CompilerParams(vmem_limit_bytes=8 * 1024 * 1024),
    )(*(pltpu.with_memory_space_constraint(x, pltpu.VMEM) for x in (out, pg)))


def solution(mesh):
    spec = P(("dp", "resp"), None)
    return jax.shard_map(
        per_device, mesh=mesh, in_specs=(spec,) * 7, out_specs=(spec,) * 5, check_vma=False
    )
```

```python
import functools

import jax
import jax.numpy as jnp
from jax import lax
from jax.experimental import pallas as pl
from jax.experimental.pallas import tpu as pltpu
from jax.sharding import PartitionSpec as P

HD = 128
CHIPS = 8
SCALE = HD ** (-0.5)
LOG2E = 1.4426950408889634
MASKED = -1e30
MESH = pl.DeviceIdType.MESH
NT = (((1,), (1,)), ((), ()))
NN = (((1,), (0,)), ((), ()))
TN = (((0,), (0,)), ((), ()))
F32 = jnp.float32
BF16 = jnp.bfloat16


def mm(a, b, dims):
    return lax.dot_general(a, b, dims, preferred_element_type=F32)


SLOT = {0: 0, 2: 1, -2: 2, 1: 3, -1: 4, 3: 5, -3: 6, 4: 7, -4: 7}


def chunks_of(heads):
    if heads == 10:
        return (0, 3, 7, 10)
    return tuple(range(0, heads, 2)) + (heads,)


def kernel(
    cuts,
    len_hbm, q_hbm, k_hbm, v_hbm, co_hbm, pk_hbm, pv_hbm,
    out_ref, pg_ref,
    len_ref, pk_ref, pv_ref, q_ref, co_ref, ka_ref, va_ref,
    gat_ref, other_ref, part_ref, mid_ref, tx_ref, end_ref,
    bias_ref, e_ref, dp_ref, ds_ref, stat_ref, grad_ref,
    in_sem, swap_send, swap_recv, own_sem, grad_sem,
    ag_send, ag_recv, rs_send, rs_recv, rs_own,
):
    nc = len(cuts) - 1
    wide = cuts[-1] * HD
    me = lax.axis_index("resp")
    y = me // 2
    core = lax.rem(me, 2)
    sibling = 2 * y + (1 - core)
    mine = pl.ds(pl.multiple_of(core * wide, wide), wide)
    theirs = pl.ds(pl.multiple_of((1 - core) * wide, wide), wide)

    def away(offset, other=0):
        return 2 * lax.rem(y + CHIPS + offset, CHIPS) + (1 - core if other else core)

    def remote(src, dst, send, recv, to):
        return pltpu.make_async_remote_copy(
            src_ref=src, dst_ref=dst, send_sem=send, recv_sem=recv,
            device_id={"resp": to}, device_id_type=MESH,
        )

    def span(ch):
        return pl.ds(cuts[ch] * HD, (cuts[ch + 1] - cuts[ch]) * HD)

    def half(ch, way):
        lo, hi = cuts[ch], cuts[ch + 1]
        cut = lo + (hi - lo + ch // 2 % 2) // 2
        return pl.ds(lo * HD, (cut - lo) * HD) if way == 1 else pl.ds(cut * HD, (hi - cut) * HD)

    key_rows = (pl.ds(0, 128), pl.ds(256, 128))
    prompt_rows = pl.ds(128, 128)

    loads = [
        pltpu.make_async_copy(pk_hbm, pk_ref, in_sem.at[0]),
        pltpu.make_async_copy(pv_hbm, pv_ref, in_sem.at[1]),
        pltpu.make_async_copy(len_hbm, len_ref, in_sem.at[2]),
        pltpu.make_async_copy(k_hbm.at[:, mine], ka_ref.at[key_rows[0]], in_sem.at[3]),
        pltpu.make_async_copy(q_hbm.at[:, mine], q_ref.at[0], in_sem.at[4]),
        pltpu.make_async_copy(v_hbm.at[:, mine], va_ref.at[0], in_sem.at[5]),
        pltpu.make_async_copy(co_hbm.at[:, mine], co_ref.at[0], in_sem.at[6]),
    ]
    for load in loads:
        load.start()

    barrier = pltpu.get_barrier_semaphore()
    partners = [sibling] + [away(o, other) for o in (1, -1, 2, -2) for other in (0, 1)]
    for partner in partners:
        pl.semaphore_signal(barrier, inc=1, device_id={"resp": partner}, device_id_type=MESH)

    loads[0].wait()
    loads[1].wait()
    own = jnp.concatenate([pk_ref[...].astype(F32), pv_ref[...].astype(F32)], axis=0)
    first_core = core == 0
    gat_ref[0, 0] = jnp.where(first_core, own[:, :wide], own[:, wide:]).astype(BF16)
    other_ref[...] = jnp.where(first_core, own[:, wide:], own[:, :wide]).astype(BF16)

    pl.semaphore_wait(barrier, len(partners))

    def ag_send_own(ch, kind):
        cols = span(ch)
        for way in (1, -1):
            sem = 2 if kind == 1 else 0 if way == 1 else 1
            for other in (0, 1):
                src = other_ref.at[:, cols] if other else gat_ref.at[0, 0, :, cols]
                dst = gat_ref.at[SLOT[-way * kind], other, :, cols]
                remote(src, dst, ag_send.at[ch], ag_recv.at[ch, sem], away(way * kind, other)).start()

    def ag_far(ch):
        ag_send_own(ch, 2)

    def ag_near(ch):
        ag_send_own(ch, 1)

    def ag_second(ch):
        for way in (1, -1):
            slot = SLOT[-way * 2]
            block = gat_ref.at[slot, :, :, span(ch)]
            remote(block, block, ag_send.at[ch], ag_recv.at[ch, 0 if way == 1 else 1],
                   sibling).wait_recv()
            cols = half(ch, way)
            remote(gat_ref.at[slot, :, :, cols], gat_ref.at[SLOT[4], :, :, cols],
                   ag_send.at[ch], ag_recv.at[ch, 2], away(way * 2)).start()
            remote(block, gat_ref.at[SLOT[-way * 3], :, :, span(ch)],
                   ag_send.at[ch], ag_recv.at[ch, 2], away(way)).start()

    def ag_third(ch):
        rest = gat_ref.at[pl.ds(3, 5), :, :, span(ch)]
        remote(rest, rest, ag_send.at[ch], ag_recv.at[ch, 2], sibling).wait_recv()

    def ag_sent(ch):
        every = gat_ref.at[pl.ds(1, 7), :, :, span(ch)]
        remote(every, every, ag_send.at[ch], ag_recv.at[ch, 2], sibling).wait_send()

    own_block = remote(other_ref, gat_ref.at[0, 1], own_sem.at[0], own_sem.at[1], sibling)
    swaps = [
        remote(src, dst, swap_send.at[n], swap_recv.at[n], sibling)
        for n, (src, dst) in enumerate((
            (k_hbm.at[:, theirs], ka_ref.at[key_rows[1]]),
            (q_hbm.at[:, theirs], q_ref.at[1]),
            (v_hbm.at[:, theirs], va_ref.at[1]),
            (co_hbm.at[:, theirs], co_ref.at[1]),
            (bias_ref.at[0], bias_ref.at[1]),
        ))
    ]
    ag_far(0)
    ag_near(0)
    for ch in range(1, nc):
        ag_far(ch)
    own_block.start()
    for swap in swaps[:4]:
        swap.start()

    loads[2].wait()
    ends = [len_ref[0, 0]]
    for r in range(1, 4):
        ends.append(ends[-1] + len_ref[0, r])
    key_at = lax.broadcasted_iota(jnp.int32, (128, 128), 0)
    query_at = lax.broadcasted_iota(jnp.int32, (128, 128), 1)

    def segment_of(place):
        return sum((place >= end).astype(jnp.int32) for end in ends)

    allowed = (segment_of(key_at) == segment_of(query_at)) & (key_at <= query_at)
    allowed = allowed & (query_at < ends[3])
    bias_ref[0, 0:128] = jnp.where(allowed, 0.0, MASKED).astype(F32)
    bias_ref[0, 128:136] = jnp.where(query_at[0:8] < ends[3], 1.0, 0.0).astype(F32)
    swaps[4].start()
    for load in loads[3:]:
        load.wait()

    def in_turn(items, first, rest):
        ahead = first(*items[0])
        for n, item in enumerate(items):
            now = ahead
            if n + 1 < len(items):
                ahead = first(*items[n + 1])
            rest(*item, *now)

    def columns(h):
        return pl.ds(h * HD, HD)

    def heads(ch):
        return range(cuts[ch], cuts[ch + 1])

    def own_keys(ch, b):
        def first(h):
            cols = columns(h)
            return (mm(ka_ref[key_rows[b], cols], q_ref[b, :, cols], NT),
                    mm(va_ref[b, :, cols], co_ref[b, :, cols], NT))

        def rest(h, s, dp):
            s = s * (SCALE * LOG2E) + bias_ref[b, 0:128]
            m = jnp.max(s, axis=0, keepdims=True)
            e = jnp.exp2(s - m)
            e_ref[h, b] = e
            dp_ref[h, b] = dp
            lanes = pl.ds(b * 128, 128)
            stat_ref[h, 0:1, lanes] = m
            stat_ref[h, 1:2, lanes] = jnp.sum(e, axis=0, keepdims=True)
            stat_ref[h, 2:3, lanes] = jnp.sum(e * dp, axis=0, keepdims=True)

        in_turn([(h,) for h in heads(ch)], first, rest)

    def own_keys_0(ch):
        own_keys(ch, 0)

    def own_keys_1(ch):
        if ch == 0:
            for swap in swaps:
                swap.wait_recv()
        own_keys(ch, 1)

    def prompt_keys(ch):
        if ch == 0:
            own_block.wait_recv()
        ag_third(ch)
        live = jnp.concatenate([bias_ref[0, 128:129], bias_ref[1, 128:129]], axis=1)

        def first(h):
            cols = columns(h)
            both = gat_ref[:, :, :, cols].reshape(16, 16, HD).astype(F32)
            kp = both[:, :8].reshape(128, HD).astype(BF16)
            vp = both[:, 8:].reshape(128, HD).astype(BF16)
            ka_ref[prompt_rows, cols] = kp
            return (mm(kp, q_ref[:, :, cols].reshape(256, HD), NT),
                    mm(vp, co_ref[:, :, cols].reshape(256, HD), NT))

        def rest(h, s, dp):
            cols = columns(h)
            s = s * (SCALE * LOG2E)
            m_own = stat_ref[h, 0:1]
            m = jnp.maximum(jnp.max(s, axis=0, keepdims=True), m_own)
            e = jnp.exp2(s - m)
            a = jnp.exp2(m_own - m)
            total = jnp.sum(e, axis=0, keepdims=True) + a * stat_ref[h, 1:2]
            inv = live / total
            delta = (jnp.sum(e * dp, axis=0, keepdims=True) + a * stat_ref[h, 2:3]) * inv
            p = e * inv
            ds = (p * (dp - delta)).astype(BF16)
            ds_ref[h] = ds
            stat_ref[h, 3:4] = a * inv
            stat_ref[h, 4:5] = delta
            gk = mm(ds, q_ref[:, :, cols].reshape(256, HD), NN).reshape(16, 8, HD)
            gv = mm(p.astype(BF16), co_ref[:, :, cols].reshape(256, HD), NN).reshape(16, 8, HD)
            part_ref[:, :, :, cols] = (
                jnp.concatenate([gk, gv], axis=1).astype(BF16).reshape(CHIPS, 2, 16, HD))

        in_turn([(h,) for h in heads(ch)], first, rest)

    def give_back(ch):
        lo, size = cuts[ch] * HD, (cuts[ch + 1] - cuts[ch]) * HD
        at = pl.ds(pl.multiple_of(core * wide + lo, HD), size)
        return remote(grad_ref.at[:, :, span(ch)], out_ref.at[:, :, at],
                      grad_sem.at[0, ch], grad_sem.at[1, ch], sibling)

    def gradients(ch):
        def first(h, b):
            lanes = pl.ds(b * 128, 128)
            p = e_ref[h, b] * stat_ref[h, 3:4, lanes]
            ds = (p * (dp_ref[h, b] - stat_ref[h, 4:5, lanes])).astype(BF16)
            return p.astype(BF16), ds

        def rest(h, b, p, ds):
            cols = columns(h)
            dv = mm(p, co_ref[b, :, cols], NN).astype(BF16)
            dk = (mm(ds, q_ref[b, :, cols], NN) * SCALE).astype(BF16)
            dsp = ds_ref[h, :, pl.ds(b * 128, 128)]
            both = jnp.concatenate([ds, dsp] if b == 0 else [dsp, ds], axis=0)
            dq = (mm(both, ka_ref[pl.ds(b * 128, 256), cols], TN) * SCALE).astype(BF16)
            for n, grad in enumerate((dq, dk, dv)):
                if b == 0:
                    at = pl.ds(pl.multiple_of(core * wide + h * HD, HD), HD)
                    out_ref[n, :, at] = grad
                else:
                    grad_ref[n, :, cols] = grad

        in_turn([(h, b) for b in (1, 0) for h in heads(ch)], first, rest)
        give_back(ch).start()

    def end_at(kind, way, other):
        return 4 * other + 2 * (kind - 1) + (0 if way == 1 else 1)

    def rs_last(ch, kind, way, src):
        cols = span(ch)
        for other in (0, 1):
            remote(src.at[other, :, cols], end_ref.at[end_at(kind, way, other), :, cols],
                   rs_send.at[ch], rs_recv.at[ch, 0], away(way * kind, other)).start()

    def rs_mid(ch, kind, way):
        w = 0 if way == 1 else 1
        cols = half(ch, way) if kind == 4 else span(ch)
        return remote(part_ref.at[SLOT[way * kind], :, :, cols], mid_ref.at[w, kind - 3, :, :, cols],
                      rs_send.at[ch], rs_recv.at[ch, 2 * w + kind - 2],
                      away(way * (2 if kind == 4 else 1)))

    def rs_near(ch):
        cols = span(ch)
        return remote(part_ref.at[0, 1, :, cols], end_ref.at[8, :, cols],
                      rs_own.at[ch], rs_recv.at[ch, 0], sibling)

    def rs_first(ch):
        for way in (1, -1):
            rs_mid(ch, 4, way).start()
            rs_mid(ch, 3, way).start()
        for way in (1, -1):
            rs_last(ch, 1, way, part_ref.at[SLOT[way]])
        rs_near(ch).start()

    def rs_second(ch):
        cols = span(ch)
        for w, way in enumerate((1, -1)):
            some = half(ch, way)
            rs_mid(ch, 3, way).wait_recv()
            rs_mid(ch, 4, way).wait_recv()
            for other in (0, 1):
                total = part_ref[SLOT[way * 2], other, :, cols].astype(F32)
                total = total + mid_ref[w, 0, other, :, cols].astype(F32)
                tx_ref[w, other, :, cols] = total.astype(BF16)
                at = some.start - cols.start
                total = total[:, at:at + some.size] + mid_ref[w, 1, other, :, some].astype(F32)
                tx_ref[w, other, :, some] = total.astype(BF16)
            rs_last(ch, 2, way, tx_ref.at[w])

    def rs_third(ch):
        cols = span(ch)
        last = end_ref.at[:, :, cols]
        remote(last, last, rs_send.at[ch], rs_recv.at[ch, 0], sibling).wait_recv()
        same = part_ref[0, 0, :, cols].astype(F32)
        for n in range(4):
            same = same + end_ref[n, :, cols].astype(F32)
        other = end_ref[4, :, cols].astype(F32)
        for n in range(5, 9):
            other = other + end_ref[n, :, cols].astype(F32)
        for at, total in ((core, same), (1 - core, other)):
            total = jnp.concatenate([total[:8] * SCALE, total[8:]], axis=0)
            pg_ref[at, :, cols] = total.astype(BF16)

    def rs_sent(ch):
        every = part_ref.at[pl.ds(0, 7), :, :, span(ch)]
        remote(every, every, rs_send.at[ch], rs_recv.at[ch, 0], sibling).wait_send()
        rs_near(ch).wait_send()

    def swapped(ch):
        if ch == 0:
            own_block.wait_send()
            for swap in swaps:
                swap.wait_send()
        ag_sent(ch)

    def given(ch):
        give_back(ch).wait()

    for step, ch in (
        (own_keys_0, 0), (own_keys_0, 1), (ag_second, 0), (ag_near, 1),
        (own_keys_0, 2), (ag_second, 1), (ag_near, 2),
        (own_keys_1, 0), (ag_second, 2), (own_keys_1, 1), (own_keys_1, 2),
        (prompt_keys, 0), (rs_first, 0),
        (prompt_keys, 1), (rs_first, 1),
        (prompt_keys, 2), (rs_first, 2), (rs_second, 0), (rs_second, 1),
        (gradients, 0), (rs_second, 2), (gradients, 1), (gradients, 2),
        (swapped, 0), (swapped, 1), (swapped, 2),
        (rs_third, 0), (rs_third, 1),
        (rs_sent, 0), (rs_sent, 1), (given, 0), (given, 1),
        (rs_third, 2), (rs_sent, 2), (given, 2),
    ):
        if ch < nc:
            step(ch)


def finish(out_in, pg_in, dq, dk, dv, gk, gv, gk_ref, gv_ref, sem):
    copies = []
    for n, dst in enumerate((dq, dk, dv)):
        for part in range(4):
            rows = pl.ds(part * 32, 32)
            copies.append(pltpu.make_async_copy(out_in.at[n, rows], dst.at[rows], sem.at[n, part]))
    for copy in copies:
        copy.start()
    both = jnp.concatenate([pg_in[0].astype(F32), pg_in[1].astype(F32)], axis=1)
    gk_ref[...] = both[:8].astype(BF16)
    gv_ref[...] = both[8:].astype(BF16)
    for n, (src, dst) in enumerate(((gk_ref, gk), (gv_ref, gv))):
        copies.append(pltpu.make_async_copy(src, dst, sem.at[3, n]))
        copies[-1].start()
    for copy in copies:
        copy.wait()


def per_device(queries, keys, values, cotangent, lengths, prompt_keys, prompt_values):
    slots, width = queries.shape
    heads = width // HD // 2
    wide = heads * HD
    cuts = chunks_of(heads)
    nc = len(cuts) - 1
    anywhere = pl.BlockSpec(memory_space=pl.ANY)
    vmem = pl.BlockSpec(memory_space=pltpu.VMEM)
    dma = pltpu.SemaphoreType.DMA
    big = jax.ShapeDtypeStruct((slots, width), BF16)
    small = jax.ShapeDtypeStruct((8, width), BF16)
    out, pg = pl.pallas_call(
        functools.partial(kernel, cuts),
        out_shape=(pltpu.VMEM((3, slots, width), BF16), pltpu.VMEM((2, 16, wide), BF16)),
        in_specs=[pl.BlockSpec(memory_space=pltpu.HBM)] * 7,
        out_specs=(vmem,) * 2,
        scratch_shapes=[
            pltpu.SMEM((1, 4), jnp.int32),
            pltpu.VMEM((8, width), BF16),
            pltpu.VMEM((8, width), BF16),
            pltpu.VMEM((2, slots, wide), BF16),
            pltpu.VMEM((2, slots, wide), BF16),
            pltpu.VMEM((384, wide), BF16),
            pltpu.VMEM((2, slots, wide), BF16),
            pltpu.VMEM((CHIPS, 2, 16, wide), BF16),
            pltpu.VMEM((16, wide), BF16),
            pltpu.VMEM((CHIPS, 2, 16, wide), BF16),
            pltpu.VMEM((2, 2, 2, 16, wide), BF16),
            pltpu.VMEM((2, 2, 16, wide), BF16),
            pltpu.VMEM((9, 16, wide), BF16),
            pltpu.VMEM((2, 136, 128), F32),
            pltpu.VMEM((heads, 2, 128, 128), F32),
            pltpu.VMEM((heads, 2, 128, 128), F32),
            pltpu.VMEM((heads, 128, 256), BF16),
            pltpu.VMEM((heads, 8, 256), F32),
            pltpu.VMEM((3, slots, wide), BF16),
            dma((7,)), dma((5,)), dma((5,)), dma((2,)), dma((2, nc)),
            dma((nc,)), dma((nc, 3)), dma((nc,)), dma((nc, 5)), dma((nc,)),
        ],
        compiler_params=pltpu.CompilerParams(
            collective_id=0, has_side_effects=True, vmem_limit_bytes=40 * 1024 * 1024
        ),
    )(*(
        pltpu.with_memory_space_constraint(x, pltpu.HBM)
        for x in (lengths, queries, keys, values, cotangent, prompt_keys, prompt_values)
    ))
    return pl.pallas_call(
        finish,
        out_shape=(big, big, big, small, small),
        in_specs=[anywhere, vmem],
        out_specs=(anywhere,) * 5,
        scratch_shapes=[pltpu.VMEM((8, width), BF16), pltpu.VMEM((8, width), BF16), dma((4, 4))],
        compiler_params=pltpu.CompilerParams(vmem_limit_bytes=8 * 1024 * 1024),
    )(*(pltpu.with_memory_space_constraint(x, pltpu.VMEM) for x in (out, pg)))


def solution(mesh):
    spec = P(("dp", "resp"), None)
    return jax.shard_map(
        per_device, mesh=mesh, in_specs=(spec,) * 7, out_specs=(spec,) * 5, check_vma=False
    )
```

```python
import functools

import jax
import jax.numpy as jnp
from jax import lax
from jax.experimental import pallas as pl
from jax.experimental.pallas import tpu as pltpu
from jax.sharding import PartitionSpec as P

HD = 128
CHIPS = 8
SCALE = HD ** (-0.5)
LOG2E = 1.4426950408889634
MASKED = -1e30
MESH = pl.DeviceIdType.MESH
NT = (((1,), (1,)), ((), ()))
NN = (((1,), (0,)), ((), ()))
TN = (((0,), (0,)), ((), ()))
F32 = jnp.float32
BF16 = jnp.bfloat16


def mm(a, b, dims):
    return lax.dot_general(a, b, dims, preferred_element_type=F32)


SLOT = {0: 0, 2: 1, -2: 2, 1: 3, -1: 4, 3: 5, -3: 6, 4: 7, -4: 7}


def chunks_of(heads):
    if heads == 10:
        return (0, 3, 7, 10)
    return tuple(range(0, heads, 2)) + (heads,)


def kernel(
    cuts,
    len_hbm, q_hbm, k_hbm, v_hbm, co_hbm, pk_hbm, pv_hbm,
    out_ref, pg_ref,
    len_ref, pk_ref, pv_ref, q_ref, co_ref, ka_ref, va_ref,
    gat_ref, other_ref, part_ref, mid_ref, tx_ref, end_ref,
    bias_ref, e_ref, dp_ref, ds_ref, stat_ref, grad_ref,
    in_sem, swap_send, swap_recv, own_sem, grad_sem,
    ag_send, ag_recv, rs_send, rs_recv, rs_own,
):
    nc = len(cuts) - 1
    wide = cuts[-1] * HD
    me = lax.axis_index("resp")
    y = me // 2
    core = lax.rem(me, 2)
    sibling = 2 * y + (1 - core)
    mine = pl.ds(pl.multiple_of(core * wide, wide), wide)
    theirs = pl.ds(pl.multiple_of((1 - core) * wide, wide), wide)

    def away(offset, other=0):
        return 2 * lax.rem(y + CHIPS + offset, CHIPS) + (1 - core if other else core)

    def remote(src, dst, send, recv, to):
        return pltpu.make_async_remote_copy(
            src_ref=src, dst_ref=dst, send_sem=send, recv_sem=recv,
            device_id={"resp": to}, device_id_type=MESH,
        )

    def span(ch):
        return pl.ds(cuts[ch] * HD, (cuts[ch + 1] - cuts[ch]) * HD)

    def half(ch, way):
        lo, hi = cuts[ch], cuts[ch + 1]
        cut = lo + (hi - lo + ch // 2 % 2) // 2
        return pl.ds(lo * HD, (cut - lo) * HD) if way == 1 else pl.ds(cut * HD, (hi - cut) * HD)

    key_rows = (pl.ds(0, 128), pl.ds(256, 128))
    prompt_rows = pl.ds(128, 128)

    loads = [
        pltpu.make_async_copy(pk_hbm, pk_ref, in_sem.at[0]),
        pltpu.make_async_copy(pv_hbm, pv_ref, in_sem.at[1]),
        pltpu.make_async_copy(len_hbm, len_ref, in_sem.at[2]),
        pltpu.make_async_copy(k_hbm.at[:, mine], ka_ref.at[key_rows[0]], in_sem.at[3]),
        pltpu.make_async_copy(q_hbm.at[:, mine], q_ref.at[0], in_sem.at[4]),
        pltpu.make_async_copy(v_hbm.at[:, mine], va_ref.at[0], in_sem.at[5]),
        pltpu.make_async_copy(co_hbm.at[:, mine], co_ref.at[0], in_sem.at[6]),
    ]
    loads[0].start()
    loads[1].start()

    barrier = pltpu.get_barrier_semaphore()
    partners = [sibling] + [away(o, other) for o in (1, -1, 2, -2) for other in (0, 1)]
    for partner in partners:
        pl.semaphore_signal(barrier, inc=1, device_id={"resp": partner}, device_id_type=MESH)

    for load in loads[2:]:
        load.start()
    loads[0].wait()
    loads[1].wait()
    own = jnp.concatenate([pk_ref[...].astype(F32), pv_ref[...].astype(F32)], axis=0)
    first_core = core == 0
    gat_ref[0, 0] = jnp.where(first_core, own[:, :wide], own[:, wide:]).astype(BF16)
    other_ref[...] = jnp.where(first_core, own[:, wide:], own[:, :wide]).astype(BF16)

    pl.semaphore_wait(barrier, len(partners))

    def ag_send_own(ch, kind):
        cols = span(ch)
        for way in (1, -1):
            sem = 2 if kind == 1 else 0 if way == 1 else 1
            for other in (0, 1):
                src = other_ref.at[:, cols] if other else gat_ref.at[0, 0, :, cols]
                dst = gat_ref.at[SLOT[-way * kind], other, :, cols]
                remote(src, dst, ag_send.at[ch], ag_recv.at[ch, sem], away(way * kind, other)).start()

    def ag_far(ch):
        ag_send_own(ch, 2)

    def ag_near(ch):
        ag_send_own(ch, 1)

    def ag_second(ch):
        for way in (1, -1):
            slot = SLOT[-way * 2]
            block = gat_ref.at[slot, :, :, span(ch)]
            remote(block, block, ag_send.at[ch], ag_recv.at[ch, 0 if way == 1 else 1],
                   sibling).wait_recv()
            cols = half(ch, way)
            remote(gat_ref.at[slot, :, :, cols], gat_ref.at[SLOT[4], :, :, cols],
                   ag_send.at[ch], ag_recv.at[ch, 2], away(way * 2)).start()
            remote(block, gat_ref.at[SLOT[-way * 3], :, :, span(ch)],
                   ag_send.at[ch], ag_recv.at[ch, 2], away(way)).start()

    def ag_third(ch):
        rest = gat_ref.at[pl.ds(3, 5), :, :, span(ch)]
        remote(rest, rest, ag_send.at[ch], ag_recv.at[ch, 2], sibling).wait_recv()

    def ag_sent(ch):
        every = gat_ref.at[pl.ds(1, 7), :, :, span(ch)]
        remote(every, every, ag_send.at[ch], ag_recv.at[ch, 2], sibling).wait_send()

    own_block = remote(other_ref, gat_ref.at[0, 1], own_sem.at[0], own_sem.at[1], sibling)
    swaps = [
        remote(src, dst, swap_send.at[n], swap_recv.at[n], sibling)
        for n, (src, dst) in enumerate((
            (k_hbm.at[:, theirs], ka_ref.at[key_rows[1]]),
            (q_hbm.at[:, theirs], q_ref.at[1]),
            (v_hbm.at[:, theirs], va_ref.at[1]),
            (co_hbm.at[:, theirs], co_ref.at[1]),
            (bias_ref.at[0], bias_ref.at[1]),
        ))
    ]
    ag_far(0)
    ag_near(0)
    for ch in range(1, nc):
        ag_far(ch)
    own_block.start()
    for swap in swaps[:4]:
        swap.start()

    loads[2].wait()
    ends = [len_ref[0, 0]]
    for r in range(1, 4):
        ends.append(ends[-1] + len_ref[0, r])
    key_at = lax.broadcasted_iota(jnp.int32, (128, 128), 0)
    query_at = lax.broadcasted_iota(jnp.int32, (128, 128), 1)

    def segment_of(place):
        return sum((place >= end).astype(jnp.int32) for end in ends)

    allowed = (segment_of(key_at) == segment_of(query_at)) & (key_at <= query_at)
    allowed = allowed & (query_at < ends[3])
    bias_ref[0, 0:128] = jnp.where(allowed, 0.0, MASKED).astype(F32)
    bias_ref[0, 128:136] = jnp.where(query_at[0:8] < ends[3], 1.0, 0.0).astype(F32)
    swaps[4].start()
    for load in loads[3:]:
        load.wait()

    def in_turn(items, first, rest):
        ahead = first(*items[0])
        for n, item in enumerate(items):
            now = ahead
            if n + 1 < len(items):
                ahead = first(*items[n + 1])
            rest(*item, *now)

    def columns(h):
        return pl.ds(h * HD, HD)

    def heads(ch):
        return range(cuts[ch], cuts[ch + 1])

    def own_keys(ch, b):
        def first(h):
            cols = columns(h)
            return (mm(ka_ref[key_rows[b], cols], q_ref[b, :, cols], NT),
                    mm(va_ref[b, :, cols], co_ref[b, :, cols], NT))

        def rest(h, s, dp):
            s = s * (SCALE * LOG2E) + bias_ref[b, 0:128]
            m = jnp.max(s, axis=0, keepdims=True)
            e = jnp.exp2(s - m)
            e_ref[h, b] = e
            dp_ref[h, b] = dp
            lanes = pl.ds(b * 128, 128)
            stat_ref[h, 0:1, lanes] = m
            stat_ref[h, 1:2, lanes] = jnp.sum(e, axis=0, keepdims=True)
            stat_ref[h, 2:3, lanes] = jnp.sum(e * dp, axis=0, keepdims=True)

        in_turn([(h,) for h in heads(ch)], first, rest)

    def own_keys_0(ch):
        own_keys(ch, 0)

    def own_keys_1(ch):
        if ch == 0:
            for swap in swaps:
                swap.wait_recv()
        own_keys(ch, 1)

    def prompt_keys(ch):
        if ch == 0:
            own_block.wait_recv()
        ag_third(ch)
        live = jnp.concatenate([bias_ref[0, 128:129], bias_ref[1, 128:129]], axis=1)

        def first(h):
            cols = columns(h)
            both = gat_ref[:, :, :, cols].reshape(16, 16, HD).astype(F32)
            kp = both[:, :8].reshape(128, HD).astype(BF16)
            vp = both[:, 8:].reshape(128, HD).astype(BF16)
            ka_ref[prompt_rows, cols] = kp
            return (mm(kp, q_ref[:, :, cols].reshape(256, HD), NT),
                    mm(vp, co_ref[:, :, cols].reshape(256, HD), NT))

        def rest(h, s, dp):
            cols = columns(h)
            s = s * (SCALE * LOG2E)
            m_own = stat_ref[h, 0:1]
            m = jnp.maximum(jnp.max(s, axis=0, keepdims=True), m_own)
            e = jnp.exp2(s - m)
            a = jnp.exp2(m_own - m)
            total = jnp.sum(e, axis=0, keepdims=True) + a * stat_ref[h, 1:2]
            inv = live / total
            delta = (jnp.sum(e * dp, axis=0, keepdims=True) + a * stat_ref[h, 2:3]) * inv
            p = e * inv
            ds = (p * (dp - delta)).astype(BF16)
            ds_ref[h] = ds
            stat_ref[h, 3:4] = a * inv
            stat_ref[h, 4:5] = delta
            gk = mm(ds, q_ref[:, :, cols].reshape(256, HD), NN).reshape(16, 8, HD)
            gv = mm(p.astype(BF16), co_ref[:, :, cols].reshape(256, HD), NN).reshape(16, 8, HD)
            part_ref[:, :, :, cols] = (
                jnp.concatenate([gk, gv], axis=1).astype(BF16).reshape(CHIPS, 2, 16, HD))

        in_turn([(h,) for h in heads(ch)], first, rest)

    def give_back(ch):
        lo, size = cuts[ch] * HD, (cuts[ch + 1] - cuts[ch]) * HD
        at = pl.ds(pl.multiple_of(core * wide + lo, HD), size)
        return remote(grad_ref.at[:, :, span(ch)], out_ref.at[:, :, at],
                      grad_sem.at[0, ch], grad_sem.at[1, ch], sibling)

    def gradients(ch):
        def first(h, b):
            lanes = pl.ds(b * 128, 128)
            p = e_ref[h, b] * stat_ref[h, 3:4, lanes]
            ds = (p * (dp_ref[h, b] - stat_ref[h, 4:5, lanes])).astype(BF16)
            return p.astype(BF16), ds

        def rest(h, b, p, ds):
            cols = columns(h)
            dv = mm(p, co_ref[b, :, cols], NN).astype(BF16)
            dk = (mm(ds, q_ref[b, :, cols], NN) * SCALE).astype(BF16)
            dsp = ds_ref[h, :, pl.ds(b * 128, 128)]
            both = jnp.concatenate([ds, dsp] if b == 0 else [dsp, ds], axis=0)
            dq = (mm(both, ka_ref[pl.ds(b * 128, 256), cols], TN) * SCALE).astype(BF16)
            for n, grad in enumerate((dq, dk, dv)):
                if b == 0:
                    at = pl.ds(pl.multiple_of(core * wide + h * HD, HD), HD)
                    out_ref[n, :, at] = grad
                else:
                    grad_ref[n, :, cols] = grad

        in_turn([(h, b) for b in (1, 0) for h in heads(ch)], first, rest)
        give_back(ch).start()

    def end_at(kind, way, other):
        return 4 * other + 2 * (kind - 1) + (0 if way == 1 else 1)

    def rs_last(ch, kind, way, src):
        cols = span(ch)
        for other in (0, 1):
            remote(src.at[other, :, cols], end_ref.at[end_at(kind, way, other), :, cols],
                   rs_send.at[ch], rs_recv.at[ch, 0], away(way * kind, other)).start()

    def rs_mid(ch, kind, way):
        w = 0 if way == 1 else 1
        cols = half(ch, way) if kind == 4 else span(ch)
        return remote(part_ref.at[SLOT[way * kind], :, :, cols], mid_ref.at[w, kind - 3, :, :, cols],
                      rs_send.at[ch], rs_recv.at[ch, 2 * w + kind - 2],
                      away(way * (2 if kind == 4 else 1)))

    def rs_near(ch):
        cols = span(ch)
        return remote(part_ref.at[0, 1, :, cols], end_ref.at[8, :, cols],
                      rs_own.at[ch], rs_recv.at[ch, 0], sibling)

    def rs_first(ch):
        for way in (1, -1):
            rs_mid(ch, 4, way).start()
            rs_mid(ch, 3, way).start()

    def rs_beside(ch):
        for way in (1, -1):
            rs_last(ch, 1, way, part_ref.at[SLOT[way]])
        rs_near(ch).start()

    def rs_second(ch):
        cols = span(ch)
        for w, way in enumerate((1, -1)):
            some = half(ch, way)
            rs_mid(ch, 3, way).wait_recv()
            rs_mid(ch, 4, way).wait_recv()
            for other in (0, 1):
                total = part_ref[SLOT[way * 2], other, :, cols].astype(F32)
                total = total + mid_ref[w, 0, other, :, cols].astype(F32)
                tx_ref[w, other, :, cols] = total.astype(BF16)
                at = some.start - cols.start
                total = total[:, at:at + some.size] + mid_ref[w, 1, other, :, some].astype(F32)
                tx_ref[w, other, :, some] = total.astype(BF16)
            rs_last(ch, 2, way, tx_ref.at[w])

    def rs_third(ch):
        cols = span(ch)
        last = end_ref.at[:, :, cols]
        remote(last, last, rs_send.at[ch], rs_recv.at[ch, 0], sibling).wait_recv()
        same = part_ref[0, 0, :, cols].astype(F32)
        for n in range(4):
            same = same + end_ref[n, :, cols].astype(F32)
        other = end_ref[4, :, cols].astype(F32)
        for n in range(5, 9):
            other = other + end_ref[n, :, cols].astype(F32)
        for at, total in ((core, same), (1 - core, other)):
            total = jnp.concatenate([total[:8] * SCALE, total[8:]], axis=0)
            pg_ref[at, :, cols] = total.astype(BF16)

    def rs_sent(ch):
        every = part_ref.at[pl.ds(0, 7), :, :, span(ch)]
        remote(every, every, rs_send.at[ch], rs_recv.at[ch, 0], sibling).wait_send()
        rs_near(ch).wait_send()

    def swapped(ch):
        if ch == 0:
            own_block.wait_send()
            for swap in swaps:
                swap.wait_send()
        ag_sent(ch)

    def given(ch):
        give_back(ch).wait()

    for step, ch in (
        (own_keys_0, 0), (ag_second, 0), (ag_near, 1), (ag_second, 1), (ag_near, 2),
        (own_keys_0, 1), (ag_second, 2), (own_keys_0, 2), (own_keys_1, 0), (own_keys_1, 1),
        (prompt_keys, 0), (rs_first, 0), (own_keys_1, 2),
        (prompt_keys, 1), (rs_first, 1), (rs_beside, 0),
        (prompt_keys, 2), (rs_first, 2), (rs_second, 0), (rs_second, 1),
        (rs_beside, 1), (rs_beside, 2),
        (gradients, 0), (rs_second, 2), (gradients, 1), (gradients, 2),
        (swapped, 0), (swapped, 1), (swapped, 2),
        (rs_third, 0), (rs_third, 1),
        (rs_sent, 0), (rs_sent, 1), (given, 0), (given, 1),
        (rs_third, 2), (rs_sent, 2), (given, 2),
    ):
        if ch < nc:
            step(ch)


def finish(out_in, pg_in, dq, dk, dv, gk, gv, gk_ref, gv_ref, sem):
    copies = []
    for n, dst in enumerate((dq, dk, dv)):
        for part in range(4):
            rows = pl.ds(part * 32, 32)
            copies.append(pltpu.make_async_copy(out_in.at[n, rows], dst.at[rows], sem.at[n, part]))
    for copy in copies:
        copy.start()
    both = jnp.concatenate([pg_in[0].astype(F32), pg_in[1].astype(F32)], axis=1)
    gk_ref[...] = both[:8].astype(BF16)
    gv_ref[...] = both[8:].astype(BF16)
    for n, (src, dst) in enumerate(((gk_ref, gk), (gv_ref, gv))):
        copies.append(pltpu.make_async_copy(src, dst, sem.at[3, n]))
        copies[-1].start()
    for copy in copies:
        copy.wait()


def per_device(queries, keys, values, cotangent, lengths, prompt_keys, prompt_values):
    slots, width = queries.shape
    heads = width // HD // 2
    wide = heads * HD
    cuts = chunks_of(heads)
    nc = len(cuts) - 1
    anywhere = pl.BlockSpec(memory_space=pl.ANY)
    vmem = pl.BlockSpec(memory_space=pltpu.VMEM)
    dma = pltpu.SemaphoreType.DMA
    big = jax.ShapeDtypeStruct((slots, width), BF16)
    small = jax.ShapeDtypeStruct((8, width), BF16)
    out, pg = pl.pallas_call(
        functools.partial(kernel, cuts),
        out_shape=(pltpu.VMEM((3, slots, width), BF16), pltpu.VMEM((2, 16, wide), BF16)),
        in_specs=[pl.BlockSpec(memory_space=pltpu.HBM)] * 7,
        out_specs=(vmem,) * 2,
        scratch_shapes=[
            pltpu.SMEM((1, 4), jnp.int32),
            pltpu.VMEM((8, width), BF16),
            pltpu.VMEM((8, width), BF16),
            pltpu.VMEM((2, slots, wide), BF16),
            pltpu.VMEM((2, slots, wide), BF16),
            pltpu.VMEM((384, wide), BF16),
            pltpu.VMEM((2, slots, wide), BF16),
            pltpu.VMEM((CHIPS, 2, 16, wide), BF16),
            pltpu.VMEM((16, wide), BF16),
            pltpu.VMEM((CHIPS, 2, 16, wide), BF16),
            pltpu.VMEM((2, 2, 2, 16, wide), BF16),
            pltpu.VMEM((2, 2, 16, wide), BF16),
            pltpu.VMEM((9, 16, wide), BF16),
            pltpu.VMEM((2, 136, 128), F32),
            pltpu.VMEM((heads, 2, 128, 128), F32),
            pltpu.VMEM((heads, 2, 128, 128), F32),
            pltpu.VMEM((heads, 128, 256), BF16),
            pltpu.VMEM((heads, 8, 256), F32),
            pltpu.VMEM((3, slots, wide), BF16),
            dma((7,)), dma((5,)), dma((5,)), dma((2,)), dma((2, nc)),
            dma((nc,)), dma((nc, 3)), dma((nc,)), dma((nc, 5)), dma((nc,)),
        ],
        compiler_params=pltpu.CompilerParams(
            collective_id=0, has_side_effects=True, vmem_limit_bytes=40 * 1024 * 1024
        ),
    )(*(
        pltpu.with_memory_space_constraint(x, pltpu.HBM)
        for x in (lengths, queries, keys, values, cotangent, prompt_keys, prompt_values)
    ))
    return pl.pallas_call(
        finish,
        out_shape=(big, big, big, small, small),
        in_specs=[anywhere, vmem],
        out_specs=(anywhere,) * 5,
        scratch_shapes=[pltpu.VMEM((8, width), BF16), pltpu.VMEM((8, width), BF16), dma((4, 4))],
        compiler_params=pltpu.CompilerParams(vmem_limit_bytes=8 * 1024 * 1024),
    )(*(pltpu.with_memory_space_constraint(x, pltpu.VMEM) for x in (out, pg)))


def solution(mesh):
    spec = P(("dp", "resp"), None)
    return jax.shard_map(
        per_device, mesh=mesh, in_specs=(spec,) * 7, out_specs=(spec,) * 5, check_vma=False
    )
```

```python
import functools

import jax
import jax.numpy as jnp
from jax import lax
from jax.experimental import pallas as pl
from jax.experimental.pallas import tpu as pltpu
from jax.sharding import PartitionSpec as P

HD = 128
CHIPS = 8
SCALE = HD ** (-0.5)
LOG2E = 1.4426950408889634
MASKED = -1e30
MESH = pl.DeviceIdType.MESH
NT = (((1,), (1,)), ((), ()))
NN = (((1,), (0,)), ((), ()))
TN = (((0,), (0,)), ((), ()))
F32 = jnp.float32
BF16 = jnp.bfloat16


def mm(a, b, dims):
    return lax.dot_general(a, b, dims, preferred_element_type=F32)


SLOT = {0: 0, 2: 1, -2: 2, 1: 3, -1: 4, 3: 5, -3: 6, 4: 7, -4: 7}


def chunks_of(heads):
    if heads == 10:
        return (0, 2, 5, 8, 10)
    return tuple(range(0, heads, 2)) + (heads,)


def kernel(
    cuts,
    len_hbm, q_hbm, k_hbm, v_hbm, co_hbm, pk_hbm, pv_hbm,
    out_ref, pg_ref,
    len_ref, pk_ref, pv_ref, q_ref, co_ref, ka_ref, va_ref,
    gat_ref, other_ref, part_ref, mid_ref, tx_ref, end_ref,
    bias_ref, e_ref, dp_ref, ds_ref, stat_ref, grad_ref,
    in_sem, swap_send, swap_recv, own_sem, grad_sem,
    ag_send, ag_recv, rs_send, rs_recv, rs_own,
):
    nc = len(cuts) - 1
    wide = cuts[-1] * HD
    me = lax.axis_index("resp")
    y = me // 2
    core = lax.rem(me, 2)
    sibling = 2 * y + (1 - core)
    mine = pl.ds(pl.multiple_of(core * wide, wide), wide)
    theirs = pl.ds(pl.multiple_of((1 - core) * wide, wide), wide)

    def away(offset, other=0):
        return 2 * lax.rem(y + CHIPS + offset, CHIPS) + (1 - core if other else core)

    def remote(src, dst, send, recv, to):
        return pltpu.make_async_remote_copy(
            src_ref=src, dst_ref=dst, send_sem=send, recv_sem=recv,
            device_id={"resp": to}, device_id_type=MESH,
        )

    def span(ch):
        return pl.ds(cuts[ch] * HD, (cuts[ch + 1] - cuts[ch]) * HD)

    def half(ch, way):
        lo, hi = cuts[ch], cuts[ch + 1]
        cut = lo + (hi - lo + ch % 2) // 2
        return pl.ds(lo * HD, (cut - lo) * HD) if way == 1 else pl.ds(cut * HD, (hi - cut) * HD)

    key_rows = (pl.ds(0, 128), pl.ds(256, 128))
    prompt_rows = pl.ds(128, 128)

    loads = [
        pltpu.make_async_copy(pk_hbm, pk_ref, in_sem.at[0]),
        pltpu.make_async_copy(pv_hbm, pv_ref, in_sem.at[1]),
        pltpu.make_async_copy(len_hbm, len_ref, in_sem.at[2]),
        pltpu.make_async_copy(k_hbm.at[:, mine], ka_ref.at[key_rows[0]], in_sem.at[3]),
        pltpu.make_async_copy(q_hbm.at[:, mine], q_ref.at[0], in_sem.at[4]),
        pltpu.make_async_copy(v_hbm.at[:, mine], va_ref.at[0], in_sem.at[5]),
        pltpu.make_async_copy(co_hbm.at[:, mine], co_ref.at[0], in_sem.at[6]),
    ]
    loads[0].start()
    loads[1].start()

    barrier = pltpu.get_barrier_semaphore()
    partners = [sibling] + [away(o, other) for o in (1, -1, 2, -2) for other in (0, 1)]
    for partner in partners:
        pl.semaphore_signal(barrier, inc=1, device_id={"resp": partner}, device_id_type=MESH)

    for load in loads[2:]:
        load.start()
    loads[0].wait()
    loads[1].wait()
    own = jnp.concatenate([pk_ref[...].astype(F32), pv_ref[...].astype(F32)], axis=0)
    first_core = core == 0
    gat_ref[0, 0] = jnp.where(first_core, own[:, :wide], own[:, wide:]).astype(BF16)
    other_ref[...] = jnp.where(first_core, own[:, wide:], own[:, :wide]).astype(BF16)

    pl.semaphore_wait(barrier, len(partners))

    def ag_send_own(ch, kind):
        cols = span(ch)
        for way in (1, -1):
            sem = 2 if kind == 1 else 0 if way == 1 else 1
            if kind == 1 and ch >= 2:
                sem = 3 if way == 1 else 4
            for other in (0, 1):
                src = other_ref.at[:, cols] if other else gat_ref.at[0, 0, :, cols]
                dst = gat_ref.at[SLOT[-way * kind], other, :, cols]
                remote(src, dst, ag_send.at[ch], ag_recv.at[ch, sem], away(way * kind, other)).start()

    def ag_far(ch):
        ag_send_own(ch, 2)

    def ag_near(ch):
        ag_send_own(ch, 1)

    def ag_pass(ch):
        for way in (1, -1):
            block = gat_ref.at[SLOT[-way], :, :, span(ch)]
            remote(block, block, ag_send.at[ch], ag_recv.at[ch, 3 if way == 1 else 4],
                   sibling).wait_recv()
            remote(block, gat_ref.at[SLOT[-way * 2], :, :, span(ch)],
                   ag_send.at[ch], ag_recv.at[ch, 0 if way == 1 else 1], away(way)).start()

    def ag_second(ch):
        for way in (1, -1):
            slot = SLOT[-way * 2]
            block = gat_ref.at[slot, :, :, span(ch)]
            remote(block, block, ag_send.at[ch], ag_recv.at[ch, 0 if way == 1 else 1],
                   sibling).wait_recv()
            cols = half(ch, way)
            remote(gat_ref.at[slot, :, :, cols], gat_ref.at[SLOT[4], :, :, cols],
                   ag_send.at[ch], ag_recv.at[ch, 2], away(way * 2)).start()
            remote(block, gat_ref.at[SLOT[-way * 3], :, :, span(ch)],
                   ag_send.at[ch], ag_recv.at[ch, 2], away(way)).start()

    def ag_third(ch):
        rest = gat_ref.at[pl.ds(3, 5) if ch < 2 else pl.ds(5, 3), :, :, span(ch)]
        remote(rest, rest, ag_send.at[ch], ag_recv.at[ch, 2], sibling).wait_recv()

    def ag_sent(ch):
        every = gat_ref.at[pl.ds(1, 7), :, :, span(ch)]
        remote(every, every, ag_send.at[ch], ag_recv.at[ch, 2], sibling).wait_send()

    own_block = remote(other_ref, gat_ref.at[0, 1], own_sem.at[0], own_sem.at[1], sibling)
    swaps = [
        remote(src, dst, swap_send.at[n], swap_recv.at[n], sibling)
        for n, (src, dst) in enumerate((
            (k_hbm.at[:, theirs], ka_ref.at[key_rows[1]]),
            (q_hbm.at[:, theirs], q_ref.at[1]),
            (v_hbm.at[:, theirs], va_ref.at[1]),
            (co_hbm.at[:, theirs], co_ref.at[1]),
            (bias_ref.at[0], bias_ref.at[1]),
        ))
    ]
    ag_far(0)
    ag_near(0)
    for ch in range(1, nc):
        if ch < 2:
            ag_far(ch)
        else:
            ag_near(ch)
    own_block.start()
    for swap in swaps[:4]:
        swap.start()

    loads[2].wait()
    ends = [len_ref[0, 0]]
    for r in range(1, 4):
        ends.append(ends[-1] + len_ref[0, r])
    key_at = lax.broadcasted_iota(jnp.int32, (128, 128), 0)
    query_at = lax.broadcasted_iota(jnp.int32, (128, 128), 1)

    def segment_of(place):
        return sum((place >= end).astype(jnp.int32) for end in ends)

    allowed = (segment_of(key_at) == segment_of(query_at)) & (key_at <= query_at)
    allowed = allowed & (query_at < ends[3])
    bias_ref[0, 0:128] = jnp.where(allowed, 0.0, MASKED).astype(F32)
    bias_ref[0, 128:136] = jnp.where(query_at[0:8] < ends[3], 1.0, 0.0).astype(F32)
    swaps[4].start()
    for load in loads[3:]:
        load.wait()

    def in_turn(items, first, rest):
        ahead = first(*items[0])
        for n, item in enumerate(items):
            now = ahead
            if n + 1 < len(items):
                ahead = first(*items[n + 1])
            rest(*item, *now)

    def columns(h):
        return pl.ds(h * HD, HD)

    def heads(ch):
        return range(cuts[ch], cuts[ch + 1])

    def own_keys(ch, b):
        def first(h):
            cols = columns(h)
            return (mm(ka_ref[key_rows[b], cols], q_ref[b, :, cols], NT),
                    mm(va_ref[b, :, cols], co_ref[b, :, cols], NT))

        def rest(h, s, dp):
            s = s * (SCALE * LOG2E) + bias_ref[b, 0:128]
            m = jnp.max(s, axis=0, keepdims=True)
            e = jnp.exp2(s - m)
            e_ref[h, b] = e
            dp_ref[h, b] = dp
            lanes = pl.ds(b * 128, 128)
            stat_ref[h, 0:1, lanes] = m
            stat_ref[h, 1:2, lanes] = jnp.sum(e, axis=0, keepdims=True)
            stat_ref[h, 2:3, lanes] = jnp.sum(e * dp, axis=0, keepdims=True)

        in_turn([(h,) for h in heads(ch)], first, rest)

    def own_keys_0(ch):
        own_keys(ch, 0)

    def own_keys_1(ch):
        if ch == 0:
            for swap in swaps:
                swap.wait_recv()
        own_keys(ch, 1)

    def prompt_keys(ch):
        if ch == 0:
            own_block.wait_recv()
        ag_third(ch)
        live = jnp.concatenate([bias_ref[0, 128:129], bias_ref[1, 128:129]], axis=1)

        def first(h):
            cols = columns(h)
            both = gat_ref[:, :, :, cols].reshape(16, 16, HD).astype(F32)
            kp = both[:, :8].reshape(128, HD).astype(BF16)
            vp = both[:, 8:].reshape(128, HD).astype(BF16)
            ka_ref[prompt_rows, cols] = kp
            return (mm(kp, q_ref[:, :, cols].reshape(256, HD), NT),
                    mm(vp, co_ref[:, :, cols].reshape(256, HD), NT))

        def rest(h, s, dp):
            cols = columns(h)
            s = s * (SCALE * LOG2E)
            m_own = stat_ref[h, 0:1]
            m = jnp.maximum(jnp.max(s, axis=0, keepdims=True), m_own)
            e = jnp.exp2(s - m)
            a = jnp.exp2(m_own - m)
            total = jnp.sum(e, axis=0, keepdims=True) + a * stat_ref[h, 1:2]
            inv = live / total
            delta = (jnp.sum(e * dp, axis=0, keepdims=True) + a * stat_ref[h, 2:3]) * inv
            p = e * inv
            ds = (p * (dp - delta)).astype(BF16)
            ds_ref[h] = ds
            stat_ref[h, 3:4] = a * inv
            stat_ref[h, 4:5] = delta
            gk = mm(ds, q_ref[:, :, cols].reshape(256, HD), NN).reshape(16, 8, HD)
            gv = mm(p.astype(BF16), co_ref[:, :, cols].reshape(256, HD), NN).reshape(16, 8, HD)
            part_ref[:, :, :, cols] = (
                jnp.concatenate([gk, gv], axis=1).astype(BF16).reshape(CHIPS, 2, 16, HD))

        in_turn([(h,) for h in heads(ch)], first, rest)

    def give_back(ch):
        lo, size = cuts[ch] * HD, (cuts[ch + 1] - cuts[ch]) * HD
        at = pl.ds(pl.multiple_of(core * wide + lo, HD), size)
        return remote(grad_ref.at[:, :, span(ch)], out_ref.at[:, :, at],
                      grad_sem.at[0, ch], grad_sem.at[1, ch], sibling)

    def gradients(ch):
        def first(h, b):
            lanes = pl.ds(b * 128, 128)
            p = e_ref[h, b] * stat_ref[h, 3:4, lanes]
            ds = (p * (dp_ref[h, b] - stat_ref[h, 4:5, lanes])).astype(BF16)
            return p.astype(BF16), ds

        def rest(h, b, p, ds):
            cols = columns(h)
            dv = mm(p, co_ref[b, :, cols], NN).astype(BF16)
            dk = (mm(ds, q_ref[b, :, cols], NN) * SCALE).astype(BF16)
            dsp = ds_ref[h, :, pl.ds(b * 128, 128)]
            both = jnp.concatenate([ds, dsp] if b == 0 else [dsp, ds], axis=0)
            dq = (mm(both, ka_ref[pl.ds(b * 128, 256), cols], TN) * SCALE).astype(BF16)
            for n, grad in enumerate((dq, dk, dv)):
                if b == 0:
                    at = pl.ds(pl.multiple_of(core * wide + h * HD, HD), HD)
                    out_ref[n, :, at] = grad
                else:
                    grad_ref[n, :, cols] = grad

        in_turn([(h, b) for b in (1, 0) for h in heads(ch)], first, rest)
        give_back(ch).start()

    def end_at(kind, way, other):
        return (5 if kind == 2 else 0) + 2 * other + (0 if way == 1 else 1)

    def rs_last(ch, kind, way, src):
        cols = span(ch)
        for other in (0, 1):
            remote(src.at[other, :, cols], end_ref.at[end_at(kind, way, other), :, cols],
                   rs_send.at[ch], rs_recv.at[ch, 0], away(way * kind, other)).start()

    def rs_mid(ch, kind, way):
        w = 0 if way == 1 else 1
        cols = half(ch, way) if kind == 4 else span(ch)
        return remote(part_ref.at[SLOT[way * kind], :, :, cols], mid_ref.at[w, kind - 3, :, :, cols],
                      rs_send.at[ch], rs_recv.at[ch, 2 * w + kind - 2],
                      away(way * (2 if kind == 4 else 1)))

    def rs_near(ch):
        cols = span(ch)
        return remote(part_ref.at[0, 1, :, cols], end_ref.at[4, :, cols],
                      rs_own.at[ch], rs_recv.at[ch, 0], sibling)

    def rs_first(ch):
        for way in (1, -1):
            rs_mid(ch, 4, way).start()
            rs_mid(ch, 3, way).start()

    def rs_beside(ch):
        for way in (1, -1):
            rs_last(ch, 1, way, part_ref.at[SLOT[way]])
        rs_near(ch).start()

    def rs_second(ch):
        cols = span(ch)
        for w, way in enumerate((1, -1)):
            some = half(ch, way)
            rs_mid(ch, 3, way).wait_recv()
            rs_mid(ch, 4, way).wait_recv()
            for other in (0, 1):
                total = part_ref[SLOT[way * 2], other, :, cols].astype(F32)
                total = total + mid_ref[w, 0, other, :, cols].astype(F32)
                tx_ref[w, other, :, cols] = total.astype(BF16)
                at = some.start - cols.start
                total = total[:, at:at + some.size] + mid_ref[w, 1, other, :, some].astype(F32)
                tx_ref[w, other, :, some] = total.astype(BF16)
            if ch >= 2:
                rs_last(ch, 2, way, tx_ref.at[w])
            else:
                rs_pass_copy(ch, w, way).start()

    def rs_pass_copy(ch, w, way):
        cols = span(ch)
        return remote(tx_ref.at[w, :, :, cols], mid_ref.at[w, 2, :, :, cols],
                      rs_send.at[ch], rs_recv.at[ch, 5 + w], away(way))

    def rs_pass(ch):
        cols = span(ch)
        for w, way in enumerate((1, -1)):
            rs_pass_copy(ch, w, way).wait_recv()
            for other in (0, 1):
                total = part_ref[SLOT[way], other, :, cols].astype(F32)
                total = total + mid_ref[w, 2, other, :, cols].astype(F32)
                tx_ref[2 + w, other, :, cols] = total.astype(BF16)
            rs_last(ch, 1, way, tx_ref.at[2 + w])
        rs_near(ch).start()

    def rs_third(ch):
        cols = span(ch)
        last = end_ref.at[pl.ds(0, 9 if ch >= 2 else 5), :, cols]
        remote(last, last, rs_send.at[ch], rs_recv.at[ch, 0], sibling).wait_recv()
        same = part_ref[0, 0, :, cols].astype(F32)
        other = end_ref[4, :, cols].astype(F32)
        for n in (0, 5) if ch >= 2 else (0,):
            same = same + end_ref[n, :, cols].astype(F32) + end_ref[n + 1, :, cols].astype(F32)
            other = other + end_ref[n + 2, :, cols].astype(F32) + end_ref[n + 3, :, cols].astype(F32)
        for at, total in ((core, same), (1 - core, other)):
            total = jnp.concatenate([total[:8] * SCALE, total[8:]], axis=0)
            pg_ref[at, :, cols] = total.astype(BF16)

    def rs_sent(ch):
        every = part_ref.at[pl.ds(0, 7), :, :, span(ch)]
        remote(every, every, rs_send.at[ch], rs_recv.at[ch, 0], sibling).wait_send()
        rs_near(ch).wait_send()

    def swapped(ch):
        if ch == 0:
            own_block.wait_send()
            for swap in swaps:
                swap.wait_send()
        ag_sent(ch)

    def given(ch):
        give_back(ch).wait()

    for step, ch in (
        (own_keys_0, 0), (ag_second, 0), (ag_near, 1), (ag_pass, 2),
        (own_keys_0, 1), (ag_second, 1), (ag_pass, 3),
        (own_keys_0, 2), (ag_second, 2),
        (own_keys_0, 3), (ag_second, 3),
        (own_keys_1, 0), (own_keys_1, 1), (prompt_keys, 0), (rs_first, 0),
        (own_keys_1, 2), (prompt_keys, 1), (rs_first, 1),
        (own_keys_1, 3), (prompt_keys, 2), (rs_first, 2), (rs_beside, 2), (rs_second, 0),
        (prompt_keys, 3), (rs_first, 3), (rs_beside, 3), (rs_second, 1), (rs_pass, 0),
        (gradients, 0), (rs_second, 2), (gradients, 1), (rs_second, 3), (rs_pass, 1),
        (gradients, 2), (gradients, 3),
        (swapped, 0), (swapped, 1), (swapped, 2), (swapped, 3),
        (rs_third, 0), (rs_third, 1), (rs_third, 2),
        (rs_sent, 0), (rs_sent, 1), (rs_sent, 2), (given, 0), (given, 1), (given, 2),
        (rs_third, 3), (rs_sent, 3), (given, 3),
    ):
        if ch < nc:
            step(ch)


def finish(out_in, pg_in, dq, dk, dv, gk, gv, gk_ref, gv_ref, sem):
    copies = []
    for n, dst in enumerate((dq, dk, dv)):
        for part in range(4):
            rows = pl.ds(part * 32, 32)
            copies.append(pltpu.make_async_copy(out_in.at[n, rows], dst.at[rows], sem.at[n, part]))
    for copy in copies:
        copy.start()
    both = jnp.concatenate([pg_in[0].astype(F32), pg_in[1].astype(F32)], axis=1)
    gk_ref[...] = both[:8].astype(BF16)
    gv_ref[...] = both[8:].astype(BF16)
    for n, (src, dst) in enumerate(((gk_ref, gk), (gv_ref, gv))):
        copies.append(pltpu.make_async_copy(src, dst, sem.at[3, n]))
        copies[-1].start()
    for copy in copies:
        copy.wait()


def per_device(queries, keys, values, cotangent, lengths, prompt_keys, prompt_values):
    slots, width = queries.shape
    heads = width // HD // 2
    wide = heads * HD
    cuts = chunks_of(heads)
    nc = len(cuts) - 1
    anywhere = pl.BlockSpec(memory_space=pl.ANY)
    vmem = pl.BlockSpec(memory_space=pltpu.VMEM)
    dma = pltpu.SemaphoreType.DMA
    big = jax.ShapeDtypeStruct((slots, width), BF16)
    small = jax.ShapeDtypeStruct((8, width), BF16)
    out, pg = pl.pallas_call(
        functools.partial(kernel, cuts),
        out_shape=(pltpu.VMEM((3, slots, width), BF16), pltpu.VMEM((2, 16, wide), BF16)),
        in_specs=[pl.BlockSpec(memory_space=pltpu.HBM)] * 7,
        out_specs=(vmem,) * 2,
        scratch_shapes=[
            pltpu.SMEM((1, 4), jnp.int32),
            pltpu.VMEM((8, width), BF16),
            pltpu.VMEM((8, width), BF16),
            pltpu.VMEM((2, slots, wide), BF16),
            pltpu.VMEM((2, slots, wide), BF16),
            pltpu.VMEM((384, wide), BF16),
            pltpu.VMEM((2, slots, wide), BF16),
            pltpu.VMEM((CHIPS, 2, 16, wide), BF16),
            pltpu.VMEM((16, wide), BF16),
            pltpu.VMEM((CHIPS, 2, 16, wide), BF16),
            pltpu.VMEM((2, 3, 2, 16, wide), BF16),
            pltpu.VMEM((4, 2, 16, wide), BF16),
            pltpu.VMEM((9, 16, wide), BF16),
            pltpu.VMEM((2, 136, 128), F32),
            pltpu.VMEM((heads, 2, 128, 128), F32),
            pltpu.VMEM((heads, 2, 128, 128), F32),
            pltpu.VMEM((heads, 128, 256), BF16),
            pltpu.VMEM((heads, 8, 256), F32),
            pltpu.VMEM((3, slots, wide), BF16),
            dma((7,)), dma((5,)), dma((5,)), dma((2,)), dma((2, nc)),
            dma((nc,)), dma((nc, 5)), dma((nc,)), dma((nc, 7)), dma((nc,)),
        ],
        compiler_params=pltpu.CompilerParams(
            collective_id=0, has_side_effects=True, vmem_limit_bytes=40 * 1024 * 1024
        ),
    )(*(
        pltpu.with_memory_space_constraint(x, pltpu.HBM)
        for x in (lengths, queries, keys, values, cotangent, prompt_keys, prompt_values)
    ))
    return pl.pallas_call(
        finish,
        out_shape=(big, big, big, small, small),
        in_specs=[anywhere, vmem],
        out_specs=(anywhere,) * 5,
        scratch_shapes=[pltpu.VMEM((8, width), BF16), pltpu.VMEM((8, width), BF16), dma((4, 4))],
        compiler_params=pltpu.CompilerParams(vmem_limit_bytes=8 * 1024 * 1024),
    )(*(pltpu.with_memory_space_constraint(x, pltpu.VMEM) for x in (out, pg)))


def solution(mesh):
    spec = P(("dp", "resp"), None)
    return jax.shard_map(
        per_device, mesh=mesh, in_specs=(spec,) * 7, out_specs=(spec,) * 5, check_vma=False
    )
```

```python
import functools

import jax
import jax.numpy as jnp
from jax import lax
from jax.experimental import pallas as pl
from jax.experimental.pallas import tpu as pltpu
from jax.sharding import PartitionSpec as P

HD = 128
CHIPS = 8
SCALE = HD ** (-0.5)
LOG2E = 1.4426950408889634
MASKED = -1e30
MESH = pl.DeviceIdType.MESH
NT = (((1,), (1,)), ((), ()))
NN = (((1,), (0,)), ((), ()))
TN = (((0,), (0,)), ((), ()))
F32 = jnp.float32
BF16 = jnp.bfloat16


def mm(a, b, dims):
    return lax.dot_general(a, b, dims, preferred_element_type=F32)


SLOT = {0: 0, 2: 1, -2: 2, 1: 3, -1: 4, 3: 5, -3: 6, 4: 7, -4: 7}


def chunks_of(heads):
    if heads == 10:
        return (0, 2, 5, 8, 10)
    return tuple(range(0, heads, 2)) + (heads,)


def kernel(
    cuts,
    len_hbm, q_hbm, k_hbm, v_hbm, co_hbm, pk_hbm, pv_hbm,
    out_ref, pg_ref,
    len_ref, pk_ref, pv_ref, q_ref, co_ref, ka_ref, va_ref,
    gat_ref, other_ref, part_ref, mid_ref, tx_ref, end_ref,
    bias_ref, e_ref, dp_ref, ds_ref, stat_ref, grad_ref,
    in_sem, swap_send, swap_recv, own_sem, grad_sem,
    ag_send, ag_recv, rs_send, rs_recv, rs_own,
):
    nc = len(cuts) - 1
    wide = cuts[-1] * HD
    me = lax.axis_index("resp")
    y = me // 2
    core = lax.rem(me, 2)
    sibling = 2 * y + (1 - core)
    mine = pl.ds(pl.multiple_of(core * wide, wide), wide)
    theirs = pl.ds(pl.multiple_of((1 - core) * wide, wide), wide)

    def away(offset, other=0):
        return 2 * lax.rem(y + CHIPS + offset, CHIPS) + (1 - core if other else core)

    def remote(src, dst, send, recv, to):
        return pltpu.make_async_remote_copy(
            src_ref=src, dst_ref=dst, send_sem=send, recv_sem=recv,
            device_id={"resp": to}, device_id_type=MESH,
        )

    def span(ch):
        return pl.ds(cuts[ch] * HD, (cuts[ch + 1] - cuts[ch]) * HD)

    def half(ch, way):
        lo, hi = cuts[ch], cuts[ch + 1]
        cut = lo + (hi - lo + ch % 2) // 2
        return pl.ds(lo * HD, (cut - lo) * HD) if way == 1 else pl.ds(cut * HD, (hi - cut) * HD)

    key_rows = (pl.ds(0, 128), pl.ds(256, 128))
    prompt_rows = pl.ds(128, 128)

    loads = [
        pltpu.make_async_copy(pk_hbm, pk_ref, in_sem.at[0]),
        pltpu.make_async_copy(pv_hbm, pv_ref, in_sem.at[1]),
        pltpu.make_async_copy(len_hbm, len_ref, in_sem.at[2]),
        pltpu.make_async_copy(k_hbm.at[:, mine], ka_ref.at[key_rows[0]], in_sem.at[3]),
        pltpu.make_async_copy(q_hbm.at[:, mine], q_ref.at[0], in_sem.at[4]),
        pltpu.make_async_copy(v_hbm.at[:, mine], va_ref.at[0], in_sem.at[5]),
        pltpu.make_async_copy(co_hbm.at[:, mine], co_ref.at[0], in_sem.at[6]),
    ]
    for load in loads:
        load.start()

    barrier = pltpu.get_barrier_semaphore()
    partners = [sibling] + [away(o, other) for o in (1, -1, 2, -2) for other in (0, 1)]
    for partner in partners:
        pl.semaphore_signal(barrier, inc=1, device_id={"resp": partner}, device_id_type=MESH)

    loads[0].wait()
    loads[1].wait()
    own = jnp.concatenate([pk_ref[...].astype(F32), pv_ref[...].astype(F32)], axis=0)
    first_core = core == 0
    gat_ref[0, 0] = jnp.where(first_core, own[:, :wide], own[:, wide:]).astype(BF16)
    other_ref[...] = jnp.where(first_core, own[:, wide:], own[:, :wide]).astype(BF16)

    pl.semaphore_wait(barrier, len(partners))

    def ag_send_own(ch, kind):
        cols = span(ch)
        for way in (1, -1):
            sem = 2 if kind == 1 else 0 if way == 1 else 1
            for other in (0, 1):
                src = other_ref.at[:, cols] if other else gat_ref.at[0, 0, :, cols]
                dst = gat_ref.at[SLOT[-way * kind], other, :, cols]
                remote(src, dst, ag_send.at[ch], ag_recv.at[ch, sem], away(way * kind, other)).start()

    def ag_far(ch):
        ag_send_own(ch, 2)

    def ag_near(ch):
        ag_send_own(ch, 1)

    def ag_second(ch):
        for way in (1, -1):
            slot = SLOT[-way * 2]
            block = gat_ref.at[slot, :, :, span(ch)]
            remote(block, block, ag_send.at[ch], ag_recv.at[ch, 0 if way == 1 else 1],
                   sibling).wait_recv()
            cols = half(ch, way)
            remote(gat_ref.at[slot, :, :, cols], gat_ref.at[SLOT[4], :, :, cols],
                   ag_send.at[ch], ag_recv.at[ch, 2], away(way * 2)).start()
            remote(block, gat_ref.at[SLOT[-way * 3], :, :, span(ch)],
                   ag_send.at[ch], ag_recv.at[ch, 2], away(way)).start()

    def ag_third(ch):
        rest = gat_ref.at[pl.ds(3, 5), :, :, span(ch)]
        remote(rest, rest, ag_send.at[ch], ag_recv.at[ch, 2], sibling).wait_recv()

    def ag_sent(ch):
        every = gat_ref.at[pl.ds(1, 7), :, :, span(ch)]
        remote(every, every, ag_send.at[ch], ag_recv.at[ch, 2], sibling).wait_send()

    own_block = remote(other_ref, gat_ref.at[0, 1], own_sem.at[0], own_sem.at[1], sibling)
    swaps = [
        remote(src, dst, swap_send.at[n], swap_recv.at[n], sibling)
        for n, (src, dst) in enumerate((
            (k_hbm.at[:, theirs], ka_ref.at[key_rows[1]]),
            (q_hbm.at[:, theirs], q_ref.at[1]),
            (v_hbm.at[:, theirs], va_ref.at[1]),
            (co_hbm.at[:, theirs], co_ref.at[1]),
            (bias_ref.at[0], bias_ref.at[1]),
        ))
    ]
    ag_far(0)
    ag_near(0)
    for ch in range(1, nc):
        ag_far(ch)
    own_block.start()
    for swap in swaps[:4]:
        swap.start()

    loads[2].wait()
    ends = [len_ref[0, 0]]
    for r in range(1, 4):
        ends.append(ends[-1] + len_ref[0, r])
    key_at = lax.broadcasted_iota(jnp.int32, (128, 128), 0)
    query_at = lax.broadcasted_iota(jnp.int32, (128, 128), 1)

    def segment_of(place):
        return sum((place >= end).astype(jnp.int32) for end in ends)

    allowed = (segment_of(key_at) == segment_of(query_at)) & (key_at <= query_at)
    allowed = allowed & (query_at < ends[3])
    bias_ref[0, 0:128] = jnp.where(allowed, 0.0, MASKED).astype(F32)
    bias_ref[0, 128:136] = jnp.where(query_at[0:8] < ends[3], 1.0, 0.0).astype(F32)
    swaps[4].start()
    for load in loads[3:]:
        load.wait()

    def in_turn(items, first, rest):
        ahead = first(*items[0])
        for n, item in enumerate(items):
            now = ahead
            if n + 1 < len(items):
                ahead = first(*items[n + 1])
            rest(*item, *now)

    def columns(h):
        return pl.ds(h * HD, HD)

    def heads(ch):
        return range(cuts[ch], cuts[ch + 1])

    def own_keys(ch, b):
        def first(h):
            cols = columns(h)
            return (mm(ka_ref[key_rows[b], cols], q_ref[b, :, cols], NT),
                    mm(va_ref[b, :, cols], co_ref[b, :, cols], NT))

        def rest(h, s, dp):
            s = s * (SCALE * LOG2E) + bias_ref[b, 0:128]
            m = jnp.max(s, axis=0, keepdims=True)
            e = jnp.exp2(s - m)
            e_ref[h, b] = e
            dp_ref[h, b] = dp
            lanes = pl.ds(b * 128, 128)
            stat_ref[h, 0:1, lanes] = m
            stat_ref[h, 1:2, lanes] = jnp.sum(e, axis=0, keepdims=True)
            stat_ref[h, 2:3, lanes] = jnp.sum(e * dp, axis=0, keepdims=True)

        in_turn([(h,) for h in heads(ch)], first, rest)

    def own_keys_0(ch):
        own_keys(ch, 0)

    def own_keys_1(ch):
        if ch == 0:
            for swap in swaps:
                swap.wait_recv()
        own_keys(ch, 1)

    def prompt_keys(ch):
        if ch == 0:
            own_block.wait_recv()
        ag_third(ch)
        live = jnp.concatenate([bias_ref[0, 128:129], bias_ref[1, 128:129]], axis=1)

        def first(h):
            cols = columns(h)
            both = gat_ref[:, :, :, cols].reshape(16, 16, HD).astype(F32)
            kp = both[:, :8].reshape(128, HD).astype(BF16)
            vp = both[:, 8:].reshape(128, HD).astype(BF16)
            ka_ref[prompt_rows, cols] = kp
            return (mm(kp, q_ref[:, :, cols].reshape(256, HD), NT),
                    mm(vp, co_ref[:, :, cols].reshape(256, HD), NT))

        def rest(h, s, dp):
            cols = columns(h)
            s = s * (SCALE * LOG2E)
            m_own = stat_ref[h, 0:1]
            m = jnp.maximum(jnp.max(s, axis=0, keepdims=True), m_own)
            e = jnp.exp2(s - m)
            a = jnp.exp2(m_own - m)
            total = jnp.sum(e, axis=0, keepdims=True) + a * stat_ref[h, 1:2]
            inv = live / total
            delta = (jnp.sum(e * dp, axis=0, keepdims=True) + a * stat_ref[h, 2:3]) * inv
            p = e * inv
            ds = (p * (dp - delta)).astype(BF16)
            ds_ref[h] = ds
            stat_ref[h, 3:4] = a * inv
            stat_ref[h, 4:5] = delta
            gk = mm(ds, q_ref[:, :, cols].reshape(256, HD), NN).reshape(16, 8, HD)
            gv = mm(p.astype(BF16), co_ref[:, :, cols].reshape(256, HD), NN).reshape(16, 8, HD)
            part_ref[:, :, :, cols] = (
                jnp.concatenate([gk, gv], axis=1).astype(BF16).reshape(CHIPS, 2, 16, HD))

        in_turn([(h,) for h in heads(ch)], first, rest)

    def give_back(ch):
        lo, size = cuts[ch] * HD, (cuts[ch + 1] - cuts[ch]) * HD
        at = pl.ds(pl.multiple_of(core * wide + lo, HD), size)
        return remote(grad_ref.at[:, :, span(ch)], out_ref.at[:, :, at],
                      grad_sem.at[0, ch], grad_sem.at[1, ch], sibling)

    def gradients(ch):
        def first(h, b):
            lanes = pl.ds(b * 128, 128)
            p = e_ref[h, b] * stat_ref[h, 3:4, lanes]
            ds = (p * (dp_ref[h, b] - stat_ref[h, 4:5, lanes])).astype(BF16)
            return p.astype(BF16), ds

        def rest(h, b, p, ds):
            cols = columns(h)
            dv = mm(p, co_ref[b, :, cols], NN).astype(BF16)
            dk = (mm(ds, q_ref[b, :, cols], NN) * SCALE).astype(BF16)
            dsp = ds_ref[h, :, pl.ds(b * 128, 128)]
            both = jnp.concatenate([ds, dsp] if b == 0 else [dsp, ds], axis=0)
            dq = (mm(both, ka_ref[pl.ds(b * 128, 256), cols], TN) * SCALE).astype(BF16)
            for n, grad in enumerate((dq, dk, dv)):
                if b == 0:
                    at = pl.ds(pl.multiple_of(core * wide + h * HD, HD), HD)
                    out_ref[n, :, at] = grad
                else:
                    grad_ref[n, :, cols] = grad

        in_turn([(h, b) for b in (1, 0) for h in heads(ch)], first, rest)
        give_back(ch).start()

    def end_at(kind, way, other):
        return 4 * other + 2 * (kind - 1) + (0 if way == 1 else 1)

    def rs_last(ch, kind, way, src):
        cols = span(ch)
        for other in (0, 1):
            remote(src.at[other, :, cols], end_ref.at[end_at(kind, way, other), :, cols],
                   rs_send.at[ch], rs_recv.at[ch, 0], away(way * kind, other)).start()

    def rs_mid(ch, kind, way):
        w = 0 if way == 1 else 1
        cols = half(ch, way) if kind == 4 else span(ch)
        return remote(part_ref.at[SLOT[way * kind], :, :, cols], mid_ref.at[w, kind - 3, :, :, cols],
                      rs_send.at[ch], rs_recv.at[ch, 2 * w + kind - 2],
                      away(way * (2 if kind == 4 else 1)))

    def rs_near(ch):
        cols = span(ch)
        return remote(part_ref.at[0, 1, :, cols], end_ref.at[8, :, cols],
                      rs_own.at[ch], rs_recv.at[ch, 0], sibling)

    def rs_first(ch):
        for way in (1, -1):
            rs_mid(ch, 4, way).start()
            rs_mid(ch, 3, way).start()
        for way in (1, -1):
            rs_last(ch, 1, way, part_ref.at[SLOT[way]])
        rs_near(ch).start()

    def rs_second(ch):
        cols = span(ch)
        for w, way in enumerate((1, -1)):
            some = half(ch, way)
            rs_mid(ch, 3, way).wait_recv()
            rs_mid(ch, 4, way).wait_recv()
            for other in (0, 1):
                total = part_ref[SLOT[way * 2], other, :, cols].astype(F32)
                total = total + mid_ref[w, 0, other, :, cols].astype(F32)
                tx_ref[w, other, :, cols] = total.astype(BF16)
                at = some.start - cols.start
                total = total[:, at:at + some.size] + mid_ref[w, 1, other, :, some].astype(F32)
                tx_ref[w, other, :, some] = total.astype(BF16)
            rs_last(ch, 2, way, tx_ref.at[w])

    def rs_third(ch):
        cols = span(ch)
        last = end_ref.at[:, :, cols]
        remote(last, last, rs_send.at[ch], rs_recv.at[ch, 0], sibling).wait_recv()
        same = part_ref[0, 0, :, cols].astype(F32)
        for n in range(4):
            same = same + end_ref[n, :, cols].astype(F32)
        other = end_ref[4, :, cols].astype(F32)
        for n in range(5, 9):
            other = other + end_ref[n, :, cols].astype(F32)
        for at, total in ((core, same), (1 - core, other)):
            total = jnp.concatenate([total[:8] * SCALE, total[8:]], axis=0)
            pg_ref[at, :, cols] = total.astype(BF16)

    def rs_sent(ch):
        every = part_ref.at[pl.ds(0, 7), :, :, span(ch)]
        remote(every, every, rs_send.at[ch], rs_recv.at[ch, 0], sibling).wait_send()
        rs_near(ch).wait_send()

    def swapped(ch):
        if ch == 0:
            own_block.wait_send()
            for swap in swaps:
                swap.wait_send()
        ag_sent(ch)

    def given(ch):
        give_back(ch).wait()

    for step, ch in (
        (own_keys_0, 0), (own_keys_0, 1), (ag_second, 0), (ag_near, 1),
        (own_keys_0, 2), (ag_second, 1), (ag_near, 2),
        (own_keys_0, 3), (ag_second, 2), (ag_near, 3),
        (own_keys_1, 0), (ag_second, 3),
        (own_keys_1, 1), (prompt_keys, 0), (rs_first, 0),
        (own_keys_1, 2), (prompt_keys, 1), (rs_first, 1),
        (own_keys_1, 3), (prompt_keys, 2), (rs_first, 2), (rs_second, 0),
        (prompt_keys, 3), (rs_first, 3), (rs_second, 1),
        (gradients, 0), (rs_second, 2), (gradients, 1), (rs_second, 3),
        (gradients, 2), (gradients, 3),
        (swapped, 0), (swapped, 1), (swapped, 2), (swapped, 3),
        (rs_third, 0), (rs_third, 1), (rs_third, 2),
        (rs_sent, 0), (rs_sent, 1), (rs_sent, 2), (given, 0), (given, 1), (given, 2),
        (rs_third, 3), (rs_sent, 3), (given, 3),
    ):
        if ch < nc:
            step(ch)


def finish(out_in, pg_in, dq, dk, dv, gk, gv, gk_ref, gv_ref, sem):
    copies = []
    for n, dst in enumerate((dq, dk, dv)):
        for part in range(4):
            rows = pl.ds(part * 32, 32)
            copies.append(pltpu.make_async_copy(out_in.at[n, rows], dst.at[rows], sem.at[n, part]))
    for copy in copies:
        copy.start()
    both = jnp.concatenate([pg_in[0].astype(F32), pg_in[1].astype(F32)], axis=1)
    gk_ref[...] = both[:8].astype(BF16)
    gv_ref[...] = both[8:].astype(BF16)
    for n, (src, dst) in enumerate(((gk_ref, gk), (gv_ref, gv))):
        copies.append(pltpu.make_async_copy(src, dst, sem.at[3, n]))
        copies[-1].start()
    for copy in copies:
        copy.wait()


def per_device(queries, keys, values, cotangent, lengths, prompt_keys, prompt_values):
    slots, width = queries.shape
    heads = width // HD // 2
    wide = heads * HD
    cuts = chunks_of(heads)
    nc = len(cuts) - 1
    anywhere = pl.BlockSpec(memory_space=pl.ANY)
    vmem = pl.BlockSpec(memory_space=pltpu.VMEM)
    dma = pltpu.SemaphoreType.DMA
    big = jax.ShapeDtypeStruct((slots, width), BF16)
    small = jax.ShapeDtypeStruct((8, width), BF16)
    out, pg = pl.pallas_call(
        functools.partial(kernel, cuts),
        out_shape=(pltpu.VMEM((3, slots, width), BF16), pltpu.VMEM((2, 16, wide), BF16)),
        in_specs=[pl.BlockSpec(memory_space=pltpu.HBM)] * 7,
        out_specs=(vmem,) * 2,
        scratch_shapes=[
            pltpu.SMEM((1, 4), jnp.int32),
            pltpu.VMEM((8, width), BF16),
            pltpu.VMEM((8, width), BF16),
            pltpu.VMEM((2, slots, wide), BF16),
            pltpu.VMEM((2, slots, wide), BF16),
            pltpu.VMEM((384, wide), BF16),
            pltpu.VMEM((2, slots, wide), BF16),
            pltpu.VMEM((CHIPS, 2, 16, wide), BF16),
            pltpu.VMEM((16, wide), BF16),
            pltpu.VMEM((CHIPS, 2, 16, wide), BF16),
            pltpu.VMEM((2, 2, 2, 16, wide), BF16),
            pltpu.VMEM((2, 2, 16, wide), BF16),
            pltpu.VMEM((9, 16, wide), BF16),
            pltpu.VMEM((2, 136, 128), F32),
            pltpu.VMEM((heads, 2, 128, 128), F32),
            pltpu.VMEM((heads, 2, 128, 128), F32),
            pltpu.VMEM((heads, 128, 256), BF16),
            pltpu.VMEM((heads, 8, 256), F32),
            pltpu.VMEM((3, slots, wide), BF16),
            dma((7,)), dma((5,)), dma((5,)), dma((2,)), dma((2, nc)),
            dma((nc,)), dma((nc, 3)), dma((nc,)), dma((nc, 5)), dma((nc,)),
        ],
        compiler_params=pltpu.CompilerParams(
            collective_id=0, has_side_effects=True, vmem_limit_bytes=40 * 1024 * 1024
        ),
    )(*(
        pltpu.with_memory_space_constraint(x, pltpu.HBM)
        for x in (lengths, queries, keys, values, cotangent, prompt_keys, prompt_values)
    ))
    return pl.pallas_call(
        finish,
        out_shape=(big, big, big, small, small),
        in_specs=[anywhere, vmem],
        out_specs=(anywhere,) * 5,
        scratch_shapes=[pltpu.VMEM((8, width), BF16), pltpu.VMEM((8, width), BF16), dma((4, 4))],
        compiler_params=pltpu.CompilerParams(vmem_limit_bytes=8 * 1024 * 1024),
    )(*(pltpu.with_memory_space_constraint(x, pltpu.VMEM) for x in (out, pg)))


def solution(mesh):
    spec = P(("dp", "resp"), None)
    return jax.shard_map(
        per_device, mesh=mesh, in_specs=(spec,) * 7, out_specs=(spec,) * 5, check_vma=False
    )
```
